32 devices in a mesh: ja: 8 (over z, core), ka: 4 (over y, x).
Axes of the slice: x: 2, y: 2, z: 4, core: 2. Of those that a mesh axis runs over, the one named last changes fastest.
Arguments:
- tensor: float32 [16, 1024, 1024], P('ka', 'ja'), may hold values from -6 to 6
- factor_one: float32 [1024, 256], replicated, may hold values from -0.1875 to 0.1875
- factor_two: bfloat16 [1024, 256], P('ja'), may hold values from -0.1875 to 0.1875
Outputs:
- gram_one: float32 [1024, 1024], P(('ja', 'ka'))
- gram_two: float32 [1024, 1024], P(('ja', 'ka'))
- reduced: float32 [16, 256, 256], P('ka', 'ja')
The draws below stay inside these ranges and needn't reach their ends.
All inputs are finite; a program needn't handle non-finite values.
Results may differ from the reference program's by a relative error of at most 0.0029.
Values may be sent and summed in bfloat16 or wider, within the bound.
No kernel may reach another device: no remote copies, remote signals or barrier semaphores. Data moves between devices by JAX's collectives and lax.ppermute only.
A program may use at most 64 MiB of HBM per device.

```python
import math
import jax
import jax.numpy as jnp
from jax import lax

N1 = 1024
N2 = 1024
R1 = 256
R2 = 256
N3 = 16


def levels(rng, shape, shards, least, top_value):
    factor_of = 1.0
    for axis_at, shards_of in shards:
        heights = jax.random.uniform(jax.random.fold_in(jax.random.fold_in(rng, 6), axis_at), (shards_of,), jnp.float32, least / len(shards), top_value / len(shards))
        factor_of = factor_of * jnp.repeat(jnp.exp(heights), shape[axis_at] // shards_of).reshape((-1,) + (1,) * (len(shape) - 1 - axis_at))
    return factor_of


def scatter_about(stream_key, shape, width, limit, shards=(), dtype=jnp.bfloat16):
    drawn = jax.random.normal(stream_key, shape, jnp.float32) * width
    if len(shards) > 0:
        drawn = levels(stream_key, shape, shards, -0.22, 0.18) * drawn
    return jnp.clip(drawn, min=-limit, max=limit).astype(dtype)


def setup_inputs(seed: int = 0) -> dict:
    arg_keys = jax.random.split(jax.random.key(seed), 4)
    return {
        "tensor": scatter_about(arg_keys[0], (N3, N2, N1), 1.0, 6.0, ((0, 4), (1, 8)), jnp.float32),
        "factor_one": scatter_about(arg_keys[1], (N1, R1), N1 ** -0.5, 0.1875, (), jnp.float32),
        "factor_two": scatter_about(arg_keys[2], (N2, R2), N2 ** -0.5, 0.1875, ((0, 8),)),
    }


def reference(tensor, factor_one, factor_two):
    flat = tensor.reshape(N3 * N2, N1)
    gram_one = jnp.dot(flat.T, flat, precision=lax.Precision.HIGHEST, preferred_element_type=jnp.float32)
    gram_one = gram_one * (1.0 / math.sqrt(N2 * N3))
    core = jnp.dot(flat, factor_one, precision=lax.Precision.HIGHEST, preferred_element_type=jnp.float32)
    core = core.astype(jnp.bfloat16).reshape(N3, N2, R1).astype(jnp.float32)
    gram_two = jnp.einsum('kjr,klr->jl', core, core, precision=lax.Precision.HIGHEST)
    gram_two = gram_two * (1.0 / math.sqrt(N3 * R1))
    reduced = jnp.einsum('kjr,js->ksr', core, factor_two.astype(jnp.float32), precision=lax.Precision.HIGHEST)
    return (gram_one, gram_two, reduced)
```

```python
import functools
import math

import jax
import jax.numpy as jnp
from jax import lax
from jax.experimental import pallas as pl
from jax.experimental.pallas import tpu as pltpu
from jax.sharding import PartitionSpec as P

F32 = jnp.float32
BF16 = jnp.bfloat16
NT = (((1,), (1,)), ((), ()))
TN = (((0,), (0,)), ((), ()))
VMEM = pl.BlockSpec(memory_space=pltpu.VMEM)
SMEM = pl.BlockSpec(memory_space=pltpu.SMEM)


def halves(x):
    high = x.astype(BF16)
    return high, (x - high.astype(F32)).astype(BF16)


def dot3(a, b, dims):
    ah, al = a
    bh, bl = b
    dot = functools.partial(lax.dot_general, dimension_numbers=dims, preferred_element_type=F32)
    return dot(ah, bh) + (dot(ah, bl) + dot(al, bh))


def params():
    return pltpu.CompilerParams(vmem_limit_bytes=24 * 1024 * 1024)


def cost(flops, *arrays):
    moved = sum(a.size * a.dtype.itemsize for a in arrays)
    return pl.CostEstimate(flops=flops, bytes_accessed=moved, transcendentals=0)


def core_kernel(x_ref, f_ref, u_ref):
    slices, owned, width = x_ref.shape
    rank = f_ref.shape[1]
    x = halves(x_ref[...].reshape(slices * owned, width))
    core = dot3(x, halves(f_ref[...]), (((1,), (0,)), ((), ()))).astype(BF16)
    for k in range(slices):
        u_ref[:, k * rank : (k + 1) * rank] = core[k * owned : (k + 1) * owned]


def core_of(tensor, factor_one):
    slices, owned, _ = tensor.shape
    rank = factor_one.shape[1]
    out = jax.ShapeDtypeStruct((owned, slices * rank), BF16)
    return pl.pallas_call(
        core_kernel,
        out_shape=out,
        in_specs=[VMEM, VMEM],
        out_specs=VMEM,
        compiler_params=params(),
        cost_estimate=cost(6 * tensor.size * rank, tensor, factor_one, out),
        name="core",
    )(tensor, factor_one)


def gram_rows(x_ref, lhs_at, count, step):
    slices, owned, width = x_ref.shape
    right = halves(x_ref[...].reshape(slices * owned, width))
    for g in range(count):
        left = halves(x_ref[:, :, pl.ds(lhs_at(g), step)].reshape(slices * owned, step))
        yield g, dot3(left, right, TN)


def gram_away_kernel(c_ref, x_ref, away_ref):
    groups, step, _ = away_ref.shape
    other = 1 - c_ref[0]
    at = lambda g: pl.multiple_of((2 * g + other) * step, step)
    for g, rows in gram_rows(x_ref, at, groups, step):
        away_ref[g] = rows.astype(BF16)


def gram_home_kernel(c_ref, x_ref, came_ref, *outs):
    groups, step, _ = came_ref.shape
    block = step // len(outs)
    core, ka = c_ref[0], c_ref[1]
    at = lambda g: pl.multiple_of((2 * g + core) * step, step)
    total = outs[0]
    for g, rows in gram_rows(x_ref, at, groups, step):
        rows = rows + came_ref[g].astype(F32)
        for t in range(len(outs)):
            for b in range(len(outs)):
                @pl.when(ka == (b ^ t))
                def _():
                    outs[t][g] = rows[b * block : (b + 1) * block].astype(outs[t].dtype)


def gram_away(place, tensor, groups):
    width = tensor.shape[2]
    out = jax.ShapeDtypeStruct((groups, width // (2 * groups), width), BF16)
    return pl.pallas_call(
        gram_away_kernel,
        out_shape=out,
        in_specs=[SMEM, VMEM],
        out_specs=VMEM,
        compiler_params=params(),
        cost_estimate=cost(3 * tensor.size * width, tensor, out),
        name="gram_away",
    )(place, tensor)


def gram_home(place, tensor, came, count_ka):
    groups, step, width = came.shape
    shape = (groups, step // count_ka, width)
    outs = [jax.ShapeDtypeStruct(shape, F32 if t == 0 else BF16) for t in range(count_ka)]
    return pl.pallas_call(
        gram_home_kernel,
        out_shape=outs,
        in_specs=[SMEM, VMEM, VMEM],
        out_specs=[VMEM] * count_ka,
        compiler_params=params(),
        cost_estimate=cost(3 * tensor.size * width, tensor, came, *outs),
        name="gram_home",
    )(place, tensor, came)


def xor_permute(x, axis, bits):
    return lax.ppermute(x, axis, [(i, i ^ bits) for i in range(lax.axis_size(axis))])


def shards(tensor, factor_one, factor_two):
    slices, owned, width = tensor.shape
    count_ja = lax.axis_size("ja")
    count_ka = lax.axis_size("ka")
    count_z = count_ja // 2
    rank_one = factor_one.shape[1]
    rank_two = factor_two.shape[1]
    ja = lax.axis_index("ja")
    ka = lax.axis_index("ka")
    core_at, z = lax.rem(ja, 2), lax.div(ja, 2)
    place = jnp.stack([core_at, ka, z]).astype(jnp.int32)

    part = rank_two // count_ja
    cut = factor_two.reshape(owned, count_z, 2, part)
    mine = lax.dynamic_index_in_dim(cut, core_at, 2, keepdims=False)
    away = lax.dynamic_index_in_dim(cut, 1 - core_at, 2, keepdims=False)
    f2 = jnp.stack([mine, xor_permute(away, "ja", 1)])
    f2 = f2.transpose(2, 0, 1, 3)

    u = core_of(tensor, factor_one)

    got = {0: u}
    f2got = {0: lax.dynamic_index_in_dim(f2, z, 0, keepdims=False)}
    for t in range(1, count_z):
        low = t & -t
        got[t] = xor_permute(got[t ^ low], "ja", 2 * low)
        f2got[t] = xor_permute(lax.dynamic_index_in_dim(f2, z ^ t, 0, keepdims=False), "ja", 2 * t)

    step = width // count_ja
    norm_one = 1.0 / math.sqrt(owned * count_ja * slices * count_ka)
    if step % 128 == 0 and (step // count_ka) % 16 == 0:
        sent = gram_away(place, tensor, count_z)
        came = xor_permute(sent, "ja", 1)
        pieces = gram_home(place, tensor, came, count_ka)
    else:
        flat = tensor.reshape(slices * owned, width)
        local = jnp.dot(flat.T, flat, precision=lax.Precision.HIGH, preferred_element_type=F32)
        local = local.reshape(count_z, 2, step, width)
        sent = lax.dynamic_index_in_dim(local, 1 - core_at, 1, keepdims=False).astype(BF16)
        came = xor_permute(sent, "ja", 1)
        home = lax.dynamic_index_in_dim(local, core_at, 1, keepdims=False) + came.astype(F32)
        home = home.reshape(count_z, count_ka, step // count_ka, width)
        pieces = [
            lax.dynamic_index_in_dim(home, ka ^ t, 1, keepdims=False).astype(F32 if t == 0 else BF16)
            for t in range(count_ka)
        ]
    slab = pieces[0]
    for t in range(1, count_ka):
        slab = slab + xor_permute(pieces[t], "ka", t).astype(F32)
    gram_one = lax.dynamic_index_in_dim(slab, z, 0, keepdims=False)
    for t in range(1, count_z):
        piece = lax.dynamic_index_in_dim(slab, z ^ t, 0, keepdims=False).astype(BF16)
        gram_one = gram_one + xor_permute(piece, "ja", 2 * t).astype(F32)
    gram_one = gram_one * norm_one

    blocks = []
    for t in range(count_z):
        blocks += [got[t], xor_permute(got[t], "ja", 1)]
    gathered = jnp.concatenate(blocks, axis=0)
    columns = jnp.concatenate([f2got[t].reshape(2 * owned, part) for t in range(count_z)], axis=0)
    norm_two = 1.0 / math.sqrt(slices * count_ka * rank_one)
    partial_two = lax.dot_general(u, gathered, NT, preferred_element_type=F32)
    partial_two = partial_two.reshape(count_ka, owned // count_ka, count_ja * owned)
    gram_two = lax.dynamic_index_in_dim(partial_two, ka, 0, keepdims=False)
    for t in range(1, count_ka):
        piece = lax.dynamic_index_in_dim(partial_two, ka ^ t, 0, keepdims=False).astype(BF16)
        gram_two = gram_two + xor_permute(piece, "ka", t).astype(F32)
    gram_two = (gram_two * norm_two).reshape(owned // count_ka, count_ja, owned)
    order = jnp.arange(count_ja) ^ ja
    gram_two = jnp.take(gram_two, order, axis=1).reshape(owned // count_ka, count_ja * owned)
    reduced = lax.dot_general(columns, gathered, TN, preferred_element_type=F32)
    reduced = reduced.reshape(part, slices, rank_one).transpose(1, 0, 2)
    return (gram_one, gram_two, reduced)


def solution(mesh):
    in_specs = (P("ka", "ja", None), P(), P("ja", None))
    out_specs = (P(("ja", "ka"), None), P(("ja", "ka"), None), P("ka", "ja", None))
    return jax.shard_map(shards, mesh=mesh, in_specs=in_specs, out_specs=out_specs, check_vma=False)
```

```python
import functools
import math

import jax
import jax.numpy as jnp
from jax import lax
from jax.experimental import pallas as pl
from jax.experimental.pallas import tpu as pltpu
from jax.sharding import PartitionSpec as P

F32 = jnp.float32
BF16 = jnp.bfloat16
NN = (((1,), (0,)), ((), ()))
NT = (((1,), (1,)), ((), ()))
TN = (((0,), (0,)), ((), ()))
VMEM = pl.BlockSpec(memory_space=pltpu.VMEM)
SMEM = pl.BlockSpec(memory_space=pltpu.SMEM)
ANY = pl.BlockSpec(memory_space=pl.ANY)


def halves(x):
    high = x.astype(BF16)
    return high, (x - high.astype(F32)).astype(BF16)


def dot1(a, b, dims):
    return lax.dot_general(a, b, dims, preferred_element_type=F32)


def dot3(a, b, dims):
    return dot1(a[0], b[0], dims) + (dot1(a[0], b[1], dims) + dot1(a[1], b[0], dims))


def call(kernel, name, flops, outs, in_specs, *args, scratch=()):
    out_shape = [jax.ShapeDtypeStruct(s, d) for s, d in outs]
    moved = sum(a.size * a.dtype.itemsize for a in (*args, *out_shape))
    return pl.pallas_call(
        kernel,
        out_shape=out_shape,
        in_specs=in_specs,
        out_specs=[VMEM] * len(outs),
        scratch_shapes=list(scratch),
        compiler_params=pltpu.CompilerParams(vmem_limit_bytes=20 * 1024 * 1024),
        cost_estimate=pl.CostEstimate(flops=flops, bytes_accessed=moved, transcendentals=0),
        name=name,
    )(*args)


def core_kernel(x_hbm, f_hbm, u_ref, high_ref, low_ref, x_ref, f_ref, x_sem, f_sem):
    slices, owned, _ = x_ref.shape
    rank = f_ref.shape[1]
    f_copy = pltpu.make_async_copy(f_hbm, f_ref, f_sem)
    f_copy.start()
    copies = []
    for k in range(slices):
        copies.append(pltpu.make_async_copy(x_hbm.at[k], x_ref.at[k], x_sem.at[k]))
        copies[k].start()
    f_copy.wait()
    f = halves(f_ref[...])
    for k in range(slices):
        copies[k].wait()
        x = halves(x_ref[k])
        high_ref[k * owned : (k + 1) * owned] = x[0]
        low_ref[k * owned : (k + 1) * owned] = x[1]
        u_ref[:, k * rank : (k + 1) * rank] = dot3(x, f, NN).astype(BF16)


def own_columns(ref, core, groups, step):
    at = [pl.multiple_of((2 * g + core) * step, step) for g in range(groups)]
    return jnp.concatenate([ref[:, pl.ds(a, step)] for a in at], axis=1)


def gram_rows(core, high_ref, low_ref, groups, step):
    left = [own_columns(ref, core, groups, step) for ref in (high_ref, low_ref)]
    return dot3(left, (high_ref[...], low_ref[...]), TN)


def gram_away_kernel(place_ref, high_ref, low_ref, away_ref):
    groups, step, width = away_ref.shape
    rows = gram_rows(1 - place_ref[0], high_ref, low_ref, groups, step)
    away_ref[...] = rows.astype(BF16).reshape(groups, step, width)


def gram_home_kernel(place_ref, high_ref, low_ref, came_ref, *outs):
    *outs, rows_ref = outs
    groups, step, width = came_ref.shape
    block = step // len(outs)
    rows = gram_rows(place_ref[0], high_ref, low_ref, groups, step)
    rows_ref[...] = rows.reshape(groups, step, width) + came_ref[...].astype(F32)
    for t, out in enumerate(outs):
        at = pl.multiple_of((place_ref[1] ^ t) * block, block)
        out[...] = rows_ref[:, pl.ds(at, block)].astype(out.dtype)


def early_kernel(pairs, u_ref, *refs):
    blocks, columns, (gram_ref, sum_ref) = refs[: 2 * pairs], refs[2 * pairs : -2], refs[-2:]
    owned = u_ref.shape[0]
    total = None
    for i, block in enumerate(blocks):
        gram_ref[:, i * owned : (i + 1) * owned] = dot1(u_ref[...], block[...], NT)
        part = dot1(columns[i // 2][i % 2], block[...], TN)
        total = part if total is None else total + part
    sum_ref[...] = total


def late_kernel(pairs, scale, place_ref, u_ref, *refs):
    blocks, columns = refs[: 2 * pairs], refs[2 * pairs : 3 * pairs]
    gram_ref, sum_ref, *outs, reduced_ref, rows_ref = refs[3 * pairs :]
    owned = u_ref.shape[0]
    before = gram_ref.shape[1]
    slices, _, rank = reduced_ref.shape
    rows_ref[:, :before] = gram_ref[...]
    total = sum_ref[...]
    for i, block in enumerate(blocks):
        at = before + i * owned
        rows_ref[:, at : at + owned] = dot1(u_ref[...], block[...], NT)
    height = owned // len(outs)
    for t, out in enumerate(outs):
        at = pl.multiple_of((place_ref[1] ^ t) * height, height)
        out[...] = (rows_ref[pl.ds(at, height)] * scale).astype(out.dtype)
    for i, block in enumerate(blocks):
        total = total + dot1(columns[i // 2][i % 2], block[...], TN)
    for k in range(slices):
        reduced_ref[k] = total[:, k * rank : (k + 1) * rank]


def settle_kernel(order, place_ref, *refs):
    *parts, out_ref = refs
    width = out_ref.shape[1] // len(order)
    for i, b in enumerate(order):
        block = parts[0][:, i * width : (i + 1) * width]
        for part in parts[1:]:
            block = block + part[:, i * width : (i + 1) * width].astype(F32)
        at = pl.multiple_of((place_ref[2] ^ b) * width, width)
        out_ref[:, pl.ds(at, width)] = block


def xor_permute(x, axis, bits):
    return lax.ppermute(x, axis, [(i, i ^ bits) for i in range(lax.axis_size(axis))])


def pick(x, index, axis):
    return lax.dynamic_index_in_dim(x, index, axis, keepdims=False)


def after(x, *others):
    return lax.optimization_barrier((x, *others))[0]


def shards(tensor, factor_one, factor_two):
    slices, owned, width = tensor.shape
    count_ja = lax.axis_size("ja")
    count_ka = lax.axis_size("ka")
    count_z = count_ja // 2
    rank_one = factor_one.shape[1]
    rank_two = factor_two.shape[1]
    ja = lax.axis_index("ja")
    ka = lax.axis_index("ka")
    core_at, z = lax.rem(ja, 2), lax.div(ja, 2)
    place = jnp.stack([core_at, ka, ja]).astype(jnp.int32)
    step = width // count_ja
    tiled = step % 128 == 0 and owned % 128 == 0
    tiled = tiled and (step // count_ka) % 16 == 0 and (owned // count_ka) % 16 == 0
    norm_one = 1.0 / math.sqrt(owned * count_ja * slices * count_ka)
    norm_two = 1.0 / math.sqrt(slices * count_ka * rank_one)

    part = rank_two // count_ja
    cut = factor_two.reshape(owned, count_z, 2, part)
    f2 = [pick(cut, core_at, 2), xor_permute(pick(cut, 1 - core_at, 2), "ja", 1)]
    f2 = jnp.stack(f2).transpose(2, 0, 1, 3)
    f2 = [pick(f2, z ^ t, 0) for t in range(count_z)]

    u, high, low = call(
        core_kernel,
        "core",
        6 * tensor.size * rank_one,
        [
            ((owned, slices * rank_one), BF16),
            ((slices * owned, width), BF16),
            ((slices * owned, width), BF16),
        ],
        [ANY, ANY],
        tensor,
        factor_one,
        scratch=[
            pltpu.VMEM(tensor.shape, F32),
            pltpu.VMEM(factor_one.shape, F32),
            pltpu.SemaphoreType.DMA((slices,)),
            pltpu.SemaphoreType.DMA,
        ],
    )
    f2 = list(after(tuple(f2), u))

    got = {0: u}
    bits = [1 << b for b in range(count_z.bit_length() - 1)]
    for t in bits:
        got[t] = xor_permute(u, "ja", 2 * t)

    if tiled:
        (sent,) = call(
            gram_away_kernel,
            "gram_away",
            3 * tensor.size * width,
            [((count_z, step, width), BF16)],
            [SMEM, VMEM, VMEM],
            place,
            high,
            low,
        )
        came = xor_permute(sent, "ja", 1)
        shape = (count_z, step // count_ka, width)
        pieces = call(
            gram_home_kernel,
            "gram_home",
            3 * tensor.size * width,
            [(shape, F32 if t == 0 else BF16) for t in range(count_ka)],
            [SMEM, VMEM, VMEM, VMEM],
            place,
            high,
            low,
            came,
            scratch=[pltpu.VMEM(came.shape, F32)],
        )
    else:
        local = dot3((high, low), (high, low), TN).reshape(count_z, 2, step, width)
        came = xor_permute(pick(local, 1 - core_at, 1).astype(BF16), "ja", 1)
        home = pick(local, core_at, 1) + came.astype(F32)
        home = home.reshape(count_z, count_ka, step // count_ka, width)
        pieces = [pick(home, ka ^ t, 1) for t in range(count_ka)]
        pieces = [p if t == 0 else p.astype(BF16) for t, p in enumerate(pieces)]
    arrived = [xor_permute(pieces[t], "ka", t) for t in range(1, count_ka)]

    blocks = {0: (u, xor_permute(u, "ja", 1))}
    for t in bits:
        blocks[t] = (got[t], xor_permute(got[t], "ja", 1))
    for bit in reversed(bits):
        ahead = [t for t in range(count_z) if t & bit]
        moved = xor_permute(jnp.stack([f2[t] for t in ahead]), "ja", 2 * bit)
        for i, t in enumerate(ahead):
            f2[t] = moved[i]
    late = [t for t in range(count_z) if t not in blocks]
    for t in late:
        low_bit = t & -t
        got[t] = xor_permute(after(got[t ^ low_bit], pieces[0]), "ja", 2 * low_bit)
        blocks[t] = (got[t], xor_permute(got[t], "ja", 1))
    early = [t for t in blocks if t not in late]

    slab = pieces[0]
    for a in arrived:
        slab = slab + a.astype(F32)
    gram_one = pick(slab, z, 0)
    for t in range(1, count_z):
        gram_one = gram_one + xor_permute(pick(slab, z ^ t, 0).astype(BF16), "ja", 2 * t).astype(F32)
    gram_one = gram_one * norm_one

    order = [2 * t + c for t in early + late for c in range(2)]
    height = owned // count_ka
    if tiled:
        columns = slices * rank_one
        gram_part, sum_part = call(
            functools.partial(early_kernel, len(early)),
            "two_early",
            4 * len(early) * owned * columns * (owned + part),
            [((owned, 2 * len(early) * owned), F32), ((part, columns), F32)],
            [VMEM] * (1 + 3 * len(early)),
            u,
            *[b for t in early for b in blocks[t]],
            *[f2[t] for t in early],
        )
        shape = (height, count_ja * owned)
        *rows, reduced = call(
            functools.partial(late_kernel, len(late), norm_two),
            "two_late",
            4 * len(late) * owned * columns * (owned + part),
            [(shape, F32 if t == 0 else BF16) for t in range(count_ka)]
            + [((slices, part, rank_one), F32)],
            [SMEM] + [VMEM] * (3 + 3 * len(late)),
            place,
            u,
            *[b for t in late for b in blocks[t]],
            *[f2[t] for t in late],
            gram_part,
            sum_part,
            scratch=[pltpu.VMEM((owned, count_ja * owned), F32)],
        )
        rows = [rows[0]] + [xor_permute(rows[t], "ka", t) for t in range(1, count_ka)]
        (gram_two,) = call(
            functools.partial(settle_kernel, order),
            "settle",
            count_ka * rows[0].size,
            [(shape, F32)],
            [SMEM] + [VMEM] * count_ka,
            place,
            *rows,
        )
    else:
        gathered = jnp.concatenate([b for t in early + late for b in blocks[t]])
        columns = jnp.concatenate([f2[t].reshape(2 * owned, part) for t in early + late])
        rows = dot1(u, gathered, NT).reshape(count_ka, height, count_ja * owned) * norm_two
        gram_two = pick(rows, ka, 0)
        for t in range(1, count_ka):
            gram_two = gram_two + xor_permute(pick(rows, ka ^ t, 0).astype(BF16), "ka", t).astype(F32)
        places = jnp.zeros(count_ja, jnp.int32).at[jnp.array(order) ^ ja].set(jnp.arange(count_ja))
        gram_two = jnp.take(gram_two.reshape(height, count_ja, owned), places, axis=1)
        gram_two = gram_two.reshape(height, count_ja * owned)
        reduced = dot1(columns, gathered, TN).reshape(part, slices, rank_one).transpose(1, 0, 2)
    return (gram_one, gram_two, reduced)


def solution(mesh):
    in_specs = (P("ka", "ja", None), P(), P("ja", None))
    out_specs = (P(("ja", "ka"), None), P(("ja", "ka"), None), P("ka", "ja", None))
    return jax.shard_map(shards, mesh=mesh, in_specs=in_specs, out_specs=out_specs, check_vma=False)
```

```python
import functools
import math

import jax
import jax.numpy as jnp
from jax import lax
from jax.experimental import pallas as pl
from jax.experimental.pallas import tpu as pltpu
from jax.sharding import PartitionSpec as P

F32 = jnp.float32
BF16 = jnp.bfloat16
NN = (((1,), (0,)), ((), ()))
NT = (((1,), (1,)), ((), ()))
TN = (((0,), (0,)), ((), ()))
VMEM = pl.BlockSpec(memory_space=pltpu.VMEM)
SMEM = pl.BlockSpec(memory_space=pltpu.SMEM)
ANY = pl.BlockSpec(memory_space=pl.ANY)


def halves(x):
    high = x.astype(BF16)
    return high, (x - high.astype(F32)).astype(BF16)


def dot1(a, b, dims):
    return lax.dot_general(a, b, dims, preferred_element_type=F32)


def dot3(a, b, dims):
    return dot1(a[0], b[0], dims) + (dot1(a[0], b[1], dims) + dot1(a[1], b[0], dims))


def call(kernel, name, outs, in_specs, *args, scratch=(), vmem=4, flops=0):
    return pl.pallas_call(
        kernel,
        out_shape=[jax.ShapeDtypeStruct(s, d) for s, d in outs],
        in_specs=in_specs,
        out_specs=[VMEM] * len(outs),
        scratch_shapes=list(scratch),
        compiler_params=pltpu.CompilerParams(vmem_limit_bytes=vmem * 1024 * 1024),
        cost_estimate=pl.CostEstimate(flops=flops, bytes_accessed=0, transcendentals=0),
        name=name,
    )(*args)


def gram_rows(core, x_ref, groups, step, keep):
    slices, owned, width = x_ref.shape
    at = [pl.multiple_of((2 * g + core) * step, step) for g in range(groups)]
    left = [x_ref[:, :, pl.ds(a, step)].reshape(slices * owned, step) for a in at]
    left = halves(jnp.concatenate(left, axis=1))
    wide = min(256, width)
    for n in range(0, width, wide):
        right = halves(x_ref[:, :, n : n + wide].reshape(slices * owned, wide))
        keep(slice(n, n + wide), dot3(left, right, TN).reshape(groups, step, wide))


def away_kernel(place_ref, x_ref, away_ref):
    groups, step, _ = away_ref.shape

    def keep(at, rows):
        away_ref[:, :, at] = rows.astype(BF16)

    gram_rows(1 - place_ref[0], x_ref, groups, step, keep)


def core_kernel(place_ref, x_ref, f_ref, two_ref, _, near_ref, far_ref):
    slices, owned, _ = x_ref.shape
    rank = f_ref.shape[1]
    high = near_ref.shape[0] - owned
    side = lax.div(place_ref[2], 4)
    for out, here in ((near_ref, side), (far_ref, 1 - side)):
        chunk = two_ref[:, pl.ds(pl.multiple_of(here * 128, 128), 128)]
        for q in range(owned // high):
            out[owned:, q * 128 : (q + 1) * 128] = chunk[q * high : (q + 1) * high]
    f = halves(f_ref[...])
    for k in range(slices):
        core = dot3(halves(x_ref[k]), f, NN).astype(BF16)
        at = slice(k * rank, (k + 1) * rank)
        near_ref[:owned, at] = core
        far_ref[:owned, at] = core


def home_kernel(place_ref, x_ref, came_ref, _, own_ref, keep1_ref, keep2_ref, to1_ref, to2_ref, rows_ref):
    groups, step, _ = came_ref.shape
    block = own_ref.shape[1]
    lower, upper = slice(0, groups // 2), slice(groups // 2, groups)

    def keep(at, rows):
        rows_ref[...] = rows + came_ref[:, :, at].astype(F32)

        def part(chips, t):
            return rows_ref[chips, pl.ds(pl.multiple_of((place_ref[1] ^ t) * block, block), block)]

        own_ref[:, :, at] = part(slice(0, groups), 0)
        keep1_ref[:, :, at] = part(upper, 1)
        keep2_ref[:, :, at] = part(lower, 2)
        for i, t in enumerate((1, 3)):
            to1_ref[i, :, :, at] = part(lower, t).astype(BF16)
        for i, t in enumerate((2, 3)):
            to2_ref[i, :, :, at] = part(upper, t).astype(BF16)

    gram_rows(place_ref[0], x_ref, groups, step, keep)


def middle_kernel(own_ref, keep1_ref, keep2_ref, from1_ref, from2_ref, far_ref, sum_ref, to1_ref, to2_ref, on_ref):
    half = from1_ref.shape[1]
    to1_ref[...] = (keep1_ref[...] + from2_ref[1].astype(F32)).astype(BF16)
    to2_ref[...] = (keep2_ref[...] + from1_ref[1].astype(F32)).astype(BF16)
    on_ref[...] = far_ref[...]
    sum_ref[:half] = own_ref[:half] + from1_ref[0].astype(F32)
    sum_ref[half:] = own_ref[half:] + from2_ref[0].astype(F32)


def slab_kernel(place_ref, sum_ref, from1_ref, from2_ref, _, *outs):
    *outs, rows_ref = outs
    half = from1_ref.shape[0]
    rows_ref[:half] = sum_ref[:half] + from2_ref[...].astype(F32)
    rows_ref[half:] = sum_ref[half:] + from1_ref[...].astype(F32)
    for t, out in enumerate(outs):
        out[...] = rows_ref[lax.div(place_ref[2], 2) ^ t].astype(out.dtype)


def sum_kernel(scale, *refs):
    *parts, out_ref = refs
    total = parts[0][...]
    for part in parts[1:]:
        total = total + part[...].astype(F32)
    out_ref[...] = total * scale


def early_kernel(near, paired, got, far, mine_ref, other_ref):
    owned = mine_ref.shape[0]
    left = jnp.concatenate([near[:owned], paired[:owned]], axis=0)
    for t, block in enumerate((near, got, far)):
        rows = dot1(left, block[:owned], NT)
        at = slice(t * owned, (t + 1) * owned)
        mine_ref[:, at] = rows[:owned]
        other_ref[:, at] = rows[owned:].astype(BF16)


def late_kernel(near, paired, far, mine_early, other_early, mine_ref, other_ref):
    owned, before = mine_early.shape
    mine_ref[:, :before] = mine_early[...]
    other_ref[:, :before] = other_early[...]
    left = jnp.concatenate([near[:owned], paired[:owned]], axis=0)
    rows = dot1(left, far[:owned], NT)
    mine_ref[:, before:] = rows[:owned]
    other_ref[:, before:] = rows[owned:].astype(BF16)


def place_kernel(place_ref, mine, came, *outs):
    *outs, rows_ref = outs
    owned = mine.shape[0]
    for t in range(mine.shape[1] // owned):
        for core, part in enumerate((mine, came)):
            at = pl.multiple_of((place_ref[2] ^ (2 * t + core)) * owned, owned)
            rows_ref[:, pl.ds(at, owned)] = part[:, t * owned : (t + 1) * owned].astype(F32)
    height = owned // len(outs)
    for t, out in enumerate(outs):
        at = pl.multiple_of((place_ref[1] ^ t) * height, height)
        out[...] = rows_ref[pl.ds(at, height)].astype(out.dtype)


def reduced_kernel(place_ref, *refs):
    *blocks, _, mine_ref, other_ref, sum_ref = refs
    part = mine_ref.shape[0]
    high = blocks[0].shape[0] * 128 // (blocks[0].shape[1] + 128)
    owned = blocks[0].shape[0] - high
    total = None
    for block in blocks:
        chunk = [block[owned:, q * 128 : (q + 1) * 128] for q in range(owned // high)]
        value = dot1(jnp.concatenate(chunk, axis=0), block[:owned], TN)
        total = value if total is None else total + value
    sum_ref[...] = total
    for out, ja in ((mine_ref, place_ref[2]), (other_ref, place_ref[2] ^ 1)):
        out[...] = sum_ref[pl.ds(pl.multiple_of(lax.rem(ja, 4) * part, part), part)]


def add_kernel(mine, came, out_ref):
    slices, _, rank = out_ref.shape
    for k in range(slices):
        at = slice(k * rank, (k + 1) * rank)
        out_ref[k] = mine[:, at] + came[:, at]


def xor_permute(x, axis, bits):
    return lax.ppermute(x, axis, [(i, i ^ bits) for i in range(lax.axis_size(axis))])


def pick(x, index, axis):
    return lax.dynamic_index_in_dim(x, index, axis, keepdims=False)


def tiled_shards(tensor, factor_one, factor_two):
    slices, owned, width = tensor.shape
    count_ja = lax.axis_size("ja")
    count_ka = lax.axis_size("ka")
    count_z = count_ja // 2
    rank_one = factor_one.shape[1]
    part = factor_two.shape[1] // count_ja
    ja = lax.axis_index("ja")
    ka = lax.axis_index("ka")
    place = jnp.stack([lax.rem(ja, 2), ka, ja]).astype(jnp.int32)
    step = width // count_ja
    columns = slices * rank_one
    high = owned * 128 // columns
    norm_one = 1.0 / math.sqrt(owned * count_ja * slices * count_ka)
    norm_two = 1.0 / math.sqrt(slices * count_ka * rank_one)

    (away,) = call(
        away_kernel, "away", [((count_z, step, width), BF16)], [SMEM, VMEM], place, tensor, vmem=4
    )
    near, far = call(
        core_kernel,
        "core",
        [((owned + high, columns), BF16)] * 2,
        [SMEM, VMEM, VMEM, VMEM, ANY],
        place,
        tensor,
        factor_one,
        factor_two,
        away,
        vmem=4,
    )

    far2 = xor_permute(far, "ja", 4)
    got1 = xor_permute(near, "ja", 2)
    paired = xor_permute(near, "ja", 1)
    came = xor_permute(away, "ja", 1)

    shape = (count_z, step // count_ka, width)
    half = (count_z // 2, *shape[1:])
    own, keep1, keep2, to1, to2 = call(
        home_kernel,
        "home",
        [(shape, F32), (half, F32), (half, F32), ((2, *half), BF16), ((2, *half), BF16)],
        [SMEM, VMEM, VMEM, ANY],
        place,
        tensor,
        came,
        paired,
        scratch=[pltpu.VMEM((count_z, step, min(256, width)), F32)],
        vmem=6,
    )
    from1 = xor_permute(to1, "ka", 1)
    from2 = xor_permute(to2, "ka", 2)
    total, to1, to2, far2 = call(
        middle_kernel,
        "middle",
        [(shape, F32), (half, BF16), (half, BF16), (far2.shape, BF16)],
        [VMEM] * 6,
        own,
        keep1,
        keep2,
        from1,
        from2,
        far2,
    )
    from1 = xor_permute(to1, "ka", 1)
    from2 = xor_permute(to2, "ka", 2)
    far3 = xor_permute(far2, "ja", 2)
    begun = call(
        early_kernel,
        "two_early",
        [((owned, 3 * owned), F32), ((owned, 3 * owned), BF16)],
        [VMEM] * 4,
        near,
        paired,
        got1,
        far2,
    )
    sums = call(
        slab_kernel,
        "slab",
        [(shape[1:], F32 if t == 0 else BF16) for t in range(count_z)],
        [SMEM] + [VMEM] * 3 + [ANY],
        place,
        total,
        from1,
        from2,
        begun[0],
        scratch=[pltpu.VMEM(shape, F32)],
    )
    sums = [p if t == 0 else xor_permute(p, "ja", 2 * t) for t, p in enumerate(sums)]
    (gram_one,) = call(
        functools.partial(sum_kernel, norm_one), "one", [(shape[1:], F32)], [VMEM] * count_z, *sums
    )

    mine, other = call(
        late_kernel,
        "two_late",
        [((owned, 4 * owned), F32), ((owned, 4 * owned), BF16)],
        [VMEM] * 5,
        near,
        paired,
        far3,
        *begun,
    )
    other = xor_permute(other, "ja", 1)
    shape = (owned // count_ka, count_ja * owned)
    rows = call(
        place_kernel,
        "two_place",
        [(shape, F32 if t == 0 else BF16) for t in range(count_ka)],
        [SMEM] + [VMEM] * 2,
        place,
        mine,
        other,
        scratch=[pltpu.VMEM((owned, count_ja * owned), F32)],
    )
    mine, other = call(
        reduced_kernel,
        "reduced",
        [((part, columns), F32)] * 2,
        [SMEM] + [VMEM] * 4 + [ANY],
        place,
        near,
        got1,
        far2,
        far3,
        rows[0],
        scratch=[pltpu.VMEM((128, columns), F32)],
    )
    other = xor_permute(other, "ja", 1)
    (reduced,) = call(add_kernel, "add", [((slices, part, rank_one), F32)], [VMEM] * 2, mine, other)
    rows = [p if t == 0 else xor_permute(p, "ka", t) for t, p in enumerate(rows)]
    (gram_two,) = call(
        functools.partial(sum_kernel, norm_two), "two", [(shape, F32)], [VMEM] * count_ka, *rows
    )
    return (gram_one, gram_two, reduced)


def plain_shards(tensor, factor_one, factor_two):
    slices, owned, width = tensor.shape
    count_ja = lax.axis_size("ja")
    count_ka = lax.axis_size("ka")
    count_z = count_ja // 2
    rank_one = factor_one.shape[1]
    ja = lax.axis_index("ja")
    ka = lax.axis_index("ka")
    core_at, z = lax.rem(ja, 2), lax.div(ja, 2)
    step = width // count_ja
    x = halves(tensor.reshape(slices * owned, width))
    core = dot3(x, halves(factor_one), NN).astype(BF16).reshape(slices, owned, rank_one)
    u = core.transpose(1, 0, 2).reshape(owned, slices * rank_one)
    local = dot3(x, x, TN).reshape(count_z, 2, step, width)
    home = pick(local, core_at, 1)
    home = home + xor_permute(pick(local, 1 - core_at, 1).astype(BF16), "ja", 1).astype(F32)
    home = home.reshape(count_z, count_ka, step // count_ka, width)
    slab = pick(home, ka, 1)
    for t in range(1, count_ka):
        slab = slab + xor_permute(pick(home, ka ^ t, 1).astype(BF16), "ka", t).astype(F32)
    gram_one = pick(slab, z, 0)
    for t in range(1, count_z):
        gram_one = gram_one + xor_permute(pick(slab, z ^ t, 0).astype(BF16), "ja", 2 * t).astype(F32)
    gram_one = gram_one * (1.0 / math.sqrt(owned * count_ja * slices * count_ka))

    blocks = [u, xor_permute(u, "ja", 1)]
    for t in range(1, count_z):
        block = xor_permute(u, "ja", 2 * t)
        blocks += [block, xor_permute(block, "ja", 1)]
    places = jnp.arange(count_ja) ^ ja
    gathered = jnp.take(jnp.stack(blocks), places, axis=0).reshape(count_ja * owned, -1)
    rows = dot1(u, gathered, NT).reshape(count_ka, owned // count_ka, count_ja * owned)
    gram_two = pick(rows, ka, 0)
    for t in range(1, count_ka):
        gram_two = gram_two + xor_permute(pick(rows, ka ^ t, 0).astype(BF16), "ka", t).astype(F32)
    gram_two = gram_two * (1.0 / math.sqrt(slices * count_ka * rank_one))

    cut = factor_two.reshape(owned, count_ja, -1)
    two = [pick(cut, ja, 1)]
    two += [xor_permute(pick(cut, ja ^ b, 1), "ja", b) for b in range(1, count_ja)]
    two = jnp.take(jnp.stack(two), places, axis=0).reshape(count_ja * owned, -1)
    reduced = dot1(two, gathered, TN).reshape(-1, slices, rank_one).transpose(1, 0, 2)
    return (gram_one, gram_two, reduced)


def shards(tensor, factor_one, factor_two):
    slices, owned, width = tensor.shape
    count_ja = lax.axis_size("ja")
    count_ka = lax.axis_size("ka")
    step = width // count_ja
    columns = slices * factor_one.shape[1]
    tiled = count_ja == 8 and count_ka == 4 and factor_two.shape[1] == 256
    tiled = tiled and step % 128 == 0 and owned % 128 == 0
    tiled = tiled and step % (16 * count_ka) == 0 and owned % (16 * count_ka) == 0
    tiled = tiled and owned * 128 % (16 * columns) == 0 and columns % 128 == 0
    tiled = tiled and owned * 128 // columns * (columns // 128) == owned
    return (tiled_shards if tiled else plain_shards)(tensor, factor_one, factor_two)


def solution(mesh):
    in_specs = (P("ka", "ja", None), P(), P("ja", None))
    out_specs = (P(("ja", "ka"), None), P(("ja", "ka"), None), P("ka", "ja", None))
    return jax.shard_map(shards, mesh=mesh, in_specs=in_specs, out_specs=out_specs, check_vma=False)
```

```python
import functools
import math

import jax
import jax.numpy as jnp
from jax import lax
from jax.experimental import pallas as pl
from jax.experimental.pallas import tpu as pltpu
from jax.sharding import PartitionSpec as P

F32 = jnp.float32
BF16 = jnp.bfloat16
NN = (((1,), (0,)), ((), ()))
NT = (((1,), (1,)), ((), ()))
TN = (((0,), (0,)), ((), ()))
VMEM = pl.BlockSpec(memory_space=pltpu.VMEM)
SMEM = pl.BlockSpec(memory_space=pltpu.SMEM)
ANY = pl.BlockSpec(memory_space=pl.ANY)


def halves(x):
    high = x.astype(BF16)
    return high, (x - high.astype(F32)).astype(BF16)


def dot1(a, b, dims):
    return lax.dot_general(a, b, dims, preferred_element_type=F32)


def dot3(a, b, dims):
    return dot1(a[0], b[0], dims) + (dot1(a[0], b[1], dims) + dot1(a[1], b[0], dims))


def call(kernel, name, outs, in_specs, *args, scratch=(), vmem=4, flops=0):
    return pl.pallas_call(
        kernel,
        out_shape=[jax.ShapeDtypeStruct(s, d) for s, d in outs],
        in_specs=in_specs,
        out_specs=[VMEM] * len(outs),
        scratch_shapes=list(scratch),
        compiler_params=pltpu.CompilerParams(vmem_limit_bytes=vmem * 1024 * 1024),
        cost_estimate=pl.CostEstimate(flops=flops, bytes_accessed=0, transcendentals=0),
        name=name,
    )(*args)


def gram_rows(core, x_ref, groups, step, keep):
    slices, owned, width = x_ref.shape
    at = [pl.multiple_of((2 * g + core) * step, step) for g in range(groups)]
    left = [x_ref[:, :, pl.ds(a, step)].reshape(slices * owned, step) for a in at]
    left = halves(jnp.concatenate(left, axis=1))
    wide = min(256, width)
    for n in range(0, width, wide):
        right = halves(x_ref[:, :, n : n + wide].reshape(slices * owned, wide))
        keep(slice(n, n + wide), dot3(left, right, TN).reshape(groups, step, wide))


def away_kernel(place_ref, x_ref, away_ref):
    groups, step, _ = away_ref.shape

    def keep(at, rows):
        away_ref[:, :, at] = rows.astype(BF16)

    gram_rows(1 - place_ref[0], x_ref, groups, step, keep)


def core_kernel(place_ref, x_ref, f_ref, two_ref, _, near_ref, far_ref):
    slices, owned, _ = x_ref.shape
    rank = f_ref.shape[1]
    high = near_ref.shape[0] - owned
    side = lax.div(place_ref[2], 4)
    for out, here in ((near_ref, side), (far_ref, 1 - side)):
        chunk = two_ref[:, pl.ds(pl.multiple_of(here * 128, 128), 128)]
        for q in range(owned // high):
            out[owned:, q * 128 : (q + 1) * 128] = chunk[q * high : (q + 1) * high]
    f = halves(f_ref[...])
    for k in range(slices):
        core = dot3(halves(x_ref[k]), f, NN).astype(BF16)
        at = slice(k * rank, (k + 1) * rank)
        near_ref[:owned, at] = core
        far_ref[:owned, at] = core


def home_kernel(place_ref, x_ref, came_ref, _, own_ref, keep1_ref, keep2_ref, to1_ref, to2_ref, rows_ref):
    groups, step, _ = came_ref.shape
    block = own_ref.shape[1]
    lower, upper = slice(0, groups // 2), slice(groups // 2, groups)

    def keep(at, rows):
        rows_ref[...] = rows + came_ref[:, :, at].astype(F32)

        def part(chips, t):
            return rows_ref[chips, pl.ds(pl.multiple_of((place_ref[1] ^ t) * block, block), block)]

        own_ref[:, :, at] = part(slice(0, groups), 0)
        keep1_ref[:, :, at] = part(upper, 1)
        keep2_ref[:, :, at] = part(lower, 2)
        for i, t in enumerate((1, 3)):
            to1_ref[i, :, :, at] = part(lower, t).astype(BF16)
        for i, t in enumerate((2, 3)):
            to2_ref[i, :, :, at] = part(upper, t).astype(BF16)

    gram_rows(place_ref[0], x_ref, groups, step, keep)


def middle_kernel(own_ref, keep1_ref, keep2_ref, from1_ref, from2_ref, _, __, sum_ref, to1_ref, to2_ref):
    half = from1_ref.shape[1]
    to1_ref[...] = (keep1_ref[...] + from2_ref[1].astype(F32)).astype(BF16)
    to2_ref[...] = (keep2_ref[...] + from1_ref[1].astype(F32)).astype(BF16)
    sum_ref[:half] = own_ref[:half] + from1_ref[0].astype(F32)
    sum_ref[half:] = own_ref[half:] + from2_ref[0].astype(F32)


def slab_kernel(place_ref, sum_ref, from1_ref, from2_ref, _, *outs):
    *outs, rows_ref = outs
    half = from1_ref.shape[0]
    rows_ref[:half] = sum_ref[:half] + from2_ref[...].astype(F32)
    rows_ref[half:] = sum_ref[half:] + from1_ref[...].astype(F32)
    for t, out in enumerate(outs):
        out[...] = rows_ref[lax.div(place_ref[2], 2) ^ t].astype(out.dtype)


def relay_kernel(x_ref, _, *outs):
    for i, out in enumerate(outs):
        out[...] = x_ref[i * out.shape[0] : (i + 1) * out.shape[0]]


def columns_of(ref, start, owned):
    high = ref.shape[0] - start
    chunk = [ref[start:, q * 128 : (q + 1) * 128] for q in range(owned // high)]
    return jnp.concatenate(chunk, axis=0)


def early_kernel(near, paired, got, far, mine_ref, other_ref, sum_ref):
    owned = mine_ref.shape[0]
    left = jnp.concatenate([near[:owned], paired[:owned]], axis=0)
    total = None
    for t, ref in enumerate((near, got, far)):
        rows = dot1(left, ref[:owned], NT)
        at = slice(t * owned, (t + 1) * owned)
        mine_ref[:, at] = rows[:owned]
        other_ref[:, at] = rows[owned:].astype(BF16)
        value = dot1(columns_of(ref, owned, owned), ref[:owned], TN)
        total = value if total is None else total + value
    sum_ref[...] = total


def late_kernel(count, place_ref, near, paired, mine_early, other_early, sum_early, *refs):
    far = jnp.concatenate([ref[...] for ref in refs[:1]], axis=0)
    mine_ref, part_ref, other_ref, sum_ref = refs[1 + count :]
    owned, before = mine_early.shape
    half = owned // 2
    wide = mine_ref.shape[1]
    part = part_ref.shape[0]
    mine_ref[:, :before] = mine_early[...]
    left = jnp.concatenate([near[:owned], paired[:owned]], axis=0)
    rows = dot1(left, far[:owned], NT)
    mine_ref[:, before:] = rows[:owned]
    for i in range(2):
        at = slice(i * half, (i + 1) * half)
        other_ref[:half, i * wide : i * wide + before] = other_early[at]
        other_ref[:half, i * wide + before : (i + 1) * wide] = rows[owned:][at].astype(BF16)
    sum_ref[...] = sum_early[...] + dot1(columns_of(far, owned, owned), far[:owned], TN)
    part_ref[...] = sum_ref[pl.ds(pl.multiple_of(lax.rem(place_ref[2], 4) * part, part), part)]
    away = sum_ref[pl.ds(pl.multiple_of(lax.rem(place_ref[2] ^ 1, 4) * part, part), part)]
    other_ref[half : half + part], other_ref[half + part :] = halves(away)


def place_kernel(place_ref, mine, came, *outs):
    *outs, rows_ref = outs
    owned, wide = mine.shape
    half = owned // 2
    for t in range(wide // owned):
        at = pl.multiple_of((place_ref[2] ^ (2 * t)) * owned, owned)
        rows_ref[:, pl.ds(at, owned)] = mine[:, t * owned : (t + 1) * owned]
        at = pl.multiple_of((place_ref[2] ^ (2 * t + 1)) * owned, owned)
        for i in range(2):
            part = came[:half, i * wide + t * owned : i * wide + (t + 1) * owned]
            rows_ref[i * half : (i + 1) * half, pl.ds(at, owned)] = part.astype(F32)
    height = owned // len(outs)
    for t, out in enumerate(outs):
        at = pl.multiple_of((place_ref[1] ^ t) * height, height)
        out[...] = rows_ref[pl.ds(at, height)].astype(out.dtype)


def last_kernel(scales, count, mine, came, *refs):
    parts, outs = refs[: 2 * count], refs[2 * count :]
    for i, scale in enumerate(scales):
        total = parts[i * count][...]
        for part in parts[i * count + 1 : (i + 1) * count]:
            total = total + part[...].astype(F32)
        outs[i][...] = total * scale
    slices, part, rank = outs[2].shape
    for k in range(slices):
        at = slice(k * rank, (k + 1) * rank)
        low = came[came.shape[0] - part :, at].astype(F32)
        high = came[came.shape[0] - 2 * part : came.shape[0] - part, at].astype(F32)
        outs[2][k] = mine[:, at] + (high + low)


def xor_permute(x, axis, bits):
    return lax.ppermute(x, axis, [(i, i ^ bits) for i in range(lax.axis_size(axis))])


def pick(x, index, axis):
    return lax.dynamic_index_in_dim(x, index, axis, keepdims=False)


def tiled_shards(tensor, factor_one, factor_two):
    slices, owned, width = tensor.shape
    count_ja = lax.axis_size("ja")
    count_ka = lax.axis_size("ka")
    count_z = count_ja // 2
    rank_one = factor_one.shape[1]
    part = factor_two.shape[1] // count_ja
    ja = lax.axis_index("ja")
    ka = lax.axis_index("ka")
    place = jnp.stack([lax.rem(ja, 2), ka, ja]).astype(jnp.int32)
    step = width // count_ja
    columns = slices * rank_one
    high = owned * 128 // columns
    norm_one = 1.0 / math.sqrt(owned * count_ja * slices * count_ka)
    norm_two = 1.0 / math.sqrt(slices * count_ka * rank_one)

    (away,) = call(
        away_kernel, "away", [((count_z, step, width), BF16)], [SMEM, VMEM], place, tensor, vmem=4
    )
    near, far = call(
        core_kernel,
        "core",
        [((owned + high, columns), BF16)] * 2,
        [SMEM, VMEM, VMEM, VMEM, ANY],
        place,
        tensor,
        factor_one,
        factor_two,
        away,
        vmem=4,
    )

    far2 = xor_permute(far, "ja", 4)
    got1 = xor_permute(near, "ja", 2)
    paired = xor_permute(near, "ja", 1)
    came = xor_permute(away, "ja", 1)

    shape = (count_z, step // count_ka, width)
    half = (count_z // 2, *shape[1:])
    own, keep1, keep2, to1, to2 = call(
        home_kernel,
        "home",
        [(shape, F32), (half, F32), (half, F32), ((2, *half), BF16), ((2, *half), BF16)],
        [SMEM, VMEM, VMEM, ANY],
        place,
        tensor,
        came,
        paired,
        scratch=[pltpu.VMEM((count_z, step, min(256, width)), F32)],
        vmem=6,
    )
    from1 = xor_permute(to1, "ka", 1)
    from2 = xor_permute(to2, "ka", 2)
    total, to1, to2 = call(
        middle_kernel,
        "middle",
        [(shape, F32), (half, BF16), (half, BF16)],
        [VMEM] * 5 + [ANY] * 2,
        own,
        keep1,
        keep2,
        from1,
        from2,
        got1,
        far2,
    )
    from1 = xor_permute(to1, "ka", 1)
    from2 = xor_permute(to2, "ka", 2)
    far3 = call(relay_kernel, "relay", [(far.shape, BF16)], [VMEM, ANY], far2, total)
    far3 = [xor_permute(p, "ja", 2) for p in far3]
    begun = call(
        early_kernel,
        "two_early",
        [((owned, 3 * owned), F32), ((owned, 3 * owned), BF16), ((128, columns), F32)],
        [VMEM] * 4,
        near,
        paired,
        got1,
        far2,
    )
    sums = call(
        slab_kernel,
        "slab",
        [(shape[1:], F32 if t == 0 else BF16) for t in range(count_z)],
        [SMEM] + [VMEM] * 3 + [ANY],
        place,
        total,
        from1,
        from2,
        begun[0],
        scratch=[pltpu.VMEM(shape, F32)],
    )
    sums = [p if t == 0 else xor_permute(p, "ja", 2 * t) for t, p in enumerate(sums)]

    waits = sums[:1]
    mine, mine_part, other = call(
        functools.partial(late_kernel, len(waits)),
        "two_late",
        [((owned, 4 * owned), F32), ((part, columns), F32), ((owned // 2 + 2 * part, columns), BF16)],
        [SMEM] + [VMEM] * 6 + [ANY] * len(waits),
        place,
        near,
        paired,
        *begun,
        *far3,
        *waits,
        scratch=[pltpu.VMEM((128, columns), F32)],
    )
    other = xor_permute(other, "ja", 1)
    final = (owned // count_ka, count_ja * owned)
    rows = call(
        place_kernel,
        "two_place",
        [(final, F32 if t == 0 else BF16) for t in range(count_ka)],
        [SMEM] + [VMEM] * 2,
        place,
        mine,
        other,
        scratch=[pltpu.VMEM((owned, count_ja * owned), F32)],
    )
    rows = [p if t == 0 else xor_permute(p, "ka", t) for t, p in enumerate(rows)]
    return call(
        functools.partial(last_kernel, (norm_one, norm_two), count_z),
        "last",
        [(shape[1:], F32), (final, F32), ((slices, part, rank_one), F32)],
        [VMEM] * (2 + count_z + count_ka),
        mine_part,
        other,
        *sums,
        *rows,
    )


def plain_shards(tensor, factor_one, factor_two):
    slices, owned, width = tensor.shape
    count_ja = lax.axis_size("ja")
    count_ka = lax.axis_size("ka")
    count_z = count_ja // 2
    rank_one = factor_one.shape[1]
    ja = lax.axis_index("ja")
    ka = lax.axis_index("ka")
    core_at, z = lax.rem(ja, 2), lax.div(ja, 2)
    step = width // count_ja
    x = halves(tensor.reshape(slices * owned, width))
    core = dot3(x, halves(factor_one), NN).astype(BF16).reshape(slices, owned, rank_one)
    u = core.transpose(1, 0, 2).reshape(owned, slices * rank_one)
    local = dot3(x, x, TN).reshape(count_z, 2, step, width)
    home = pick(local, core_at, 1)
    home = home + xor_permute(pick(local, 1 - core_at, 1).astype(BF16), "ja", 1).astype(F32)
    home = home.reshape(count_z, count_ka, step // count_ka, width)
    slab = pick(home, ka, 1)
    for t in range(1, count_ka):
        slab = slab + xor_permute(pick(home, ka ^ t, 1).astype(BF16), "ka", t).astype(F32)
    gram_one = pick(slab, z, 0)
    for t in range(1, count_z):
        gram_one = gram_one + xor_permute(pick(slab, z ^ t, 0).astype(BF16), "ja", 2 * t).astype(F32)
    gram_one = gram_one * (1.0 / math.sqrt(owned * count_ja * slices * count_ka))

    blocks = [u, xor_permute(u, "ja", 1)]
    for t in range(1, count_z):
        block = xor_permute(u, "ja", 2 * t)
        blocks += [block, xor_permute(block, "ja", 1)]
    places = jnp.arange(count_ja) ^ ja
    gathered = jnp.take(jnp.stack(blocks), places, axis=0).reshape(count_ja * owned, -1)
    rows = dot1(u, gathered, NT).reshape(count_ka, owned // count_ka, count_ja * owned)
    gram_two = pick(rows, ka, 0)
    for t in range(1, count_ka):
        gram_two = gram_two + xor_permute(pick(rows, ka ^ t, 0).astype(BF16), "ka", t).astype(F32)
    gram_two = gram_two * (1.0 / math.sqrt(slices * count_ka * rank_one))

    cut = factor_two.reshape(owned, count_ja, -1)
    two = [pick(cut, ja, 1)]
    two += [xor_permute(pick(cut, ja ^ b, 1), "ja", b) for b in range(1, count_ja)]
    two = jnp.take(jnp.stack(two), places, axis=0).reshape(count_ja * owned, -1)
    reduced = dot1(two, gathered, TN).reshape(-1, slices, rank_one).transpose(1, 0, 2)
    return (gram_one, gram_two, reduced)


def shards(tensor, factor_one, factor_two):
    slices, owned, width = tensor.shape
    count_ja = lax.axis_size("ja")
    count_ka = lax.axis_size("ka")
    step = width // count_ja
    columns = slices * factor_one.shape[1]
    tiled = count_ja == 8 and count_ka == 4 and factor_two.shape[1] == 256
    tiled = tiled and step % 128 == 0 and owned % 128 == 0
    tiled = tiled and step % (16 * count_ka) == 0 and owned % (16 * count_ka) == 0
    tiled = tiled and owned * 128 % (16 * columns) == 0 and columns % 128 == 0
    tiled = tiled and columns == 8 * owned and owned == 128
    return (tiled_shards if tiled else plain_shards)(tensor, factor_one, factor_two)


def solution(mesh):
    in_specs = (P("ka", "ja", None), P(), P("ja", None))
    out_specs = (P(("ja", "ka"), None), P(("ja", "ka"), None), P("ka", "ja", None))
    return jax.shard_map(shards, mesh=mesh, in_specs=in_specs, out_specs=out_specs, check_vma=False)
```

```python
import functools
import math

import jax
import jax.numpy as jnp
from jax import lax
from jax.experimental import pallas as pl
from jax.experimental.pallas import tpu as pltpu
from jax.sharding import PartitionSpec as P

F32 = jnp.float32
BF16 = jnp.bfloat16
NN = (((1,), (0,)), ((), ()))
NT = (((1,), (1,)), ((), ()))
TN = (((0,), (0,)), ((), ()))
VMEM = pl.BlockSpec(memory_space=pltpu.VMEM)
ANY = pl.BlockSpec(memory_space=pl.ANY)


def halves(x):
    high = x.astype(BF16)
    return high, (x - high.astype(F32)).astype(BF16)


def dot1(a, b, dims):
    return lax.dot_general(a, b, dims, preferred_element_type=F32)


def dot3(a, b, dims):
    return dot1(a[0], b[0], dims) + (dot1(a[0], b[1], dims) + dot1(a[1], b[0], dims))


def call(kernel, name, outs, in_specs, *args, scratch=(), vmem=4, flops=0):
    return pl.pallas_call(
        kernel,
        out_shape=[jax.ShapeDtypeStruct(s, d) for s, d in outs],
        in_specs=in_specs,
        out_specs=[VMEM] * len(outs),
        scratch_shapes=list(scratch),
        compiler_params=pltpu.CompilerParams(vmem_limit_bytes=vmem * 1024 * 1024),
        cost_estimate=pl.CostEstimate(flops=flops, bytes_accessed=0, transcendentals=0),
        name=name,
    )(*args)


def position():
    ja = lax.axis_index("ja")
    return lax.rem(ja, 2), lax.div(ja, 2), lax.axis_index("ka"), ja


def gram_rows(core, x_ref, groups, step, keep):
    slices, owned, width = x_ref.shape
    at = [pl.multiple_of((2 * g + core) * step, step) for g in range(groups)]
    left = [x_ref[:, :, pl.ds(a, step)].reshape(slices * owned, step) for a in at]
    left = halves(jnp.concatenate(left, axis=1).T)
    wide = min(256, width)
    for n in range(0, width, wide):
        right = halves(x_ref[:, :, n : n + wide].reshape(slices * owned, wide))
        keep(slice(n, n + wide), dot3(left, right, NN).reshape(groups, step, wide))


def away_kernel(x_ref, away_ref):
    groups, step, _ = away_ref.shape

    def keep(at, rows):
        away_ref[:, :, at] = rows.astype(BF16)

    gram_rows(1 - position()[0], x_ref, groups, step, keep)


def core_kernel(x_ref, f_ref, two_ref, _, near_ref, far_ref):
    slices, owned, _ = x_ref.shape
    rank = f_ref.shape[1]
    high = near_ref.shape[0] - owned
    side = lax.div(position()[1], 2)
    for out, here in ((near_ref, side), (far_ref, 1 - side)):
        chunk = two_ref[:, pl.ds(pl.multiple_of(here * 128, 128), 128)]
        for q in range(owned // high):
            out[owned:, q * 128 : (q + 1) * 128] = chunk[q * high : (q + 1) * high]
    f = halves(f_ref[...])
    for k in range(slices):
        core = dot3(halves(x_ref[k]), f, NN).astype(BF16)
        at = slice(k * rank, (k + 1) * rank)
        near_ref[:owned, at] = core
        far_ref[:owned, at] = core


def home_kernel(x_ref, came_ref, _, own_ref, keep1_ref, keep2_ref, to1_ref, to2_ref, rows_ref):
    groups, step, _ = came_ref.shape
    block = own_ref.shape[1]
    lower, upper = slice(0, groups // 2), slice(groups // 2, groups)

    def keep(at, rows):
        rows_ref[...] = rows + came_ref[:, :, at].astype(F32)

        def part(chips, t):
            return rows_ref[chips, pl.ds(pl.multiple_of((position()[2] ^ t) * block, block), block)]

        own_ref[:, :, at] = part(slice(0, groups), 0)
        keep1_ref[:, :, at] = part(upper, 1)
        keep2_ref[:, :, at] = part(lower, 2)
        for i, t in enumerate((1, 3)):
            to1_ref[i, :, :, at] = part(lower, t).astype(BF16)
        for i, t in enumerate((2, 3)):
            to2_ref[i, :, :, at] = part(upper, t).astype(BF16)

    gram_rows(position()[0], x_ref, groups, step, keep)


def middle_kernel(own_ref, keep1_ref, keep2_ref, from1_ref, from2_ref, _, __, sum_ref, to1_ref, to2_ref):
    half = from1_ref.shape[1]
    to1_ref[...] = (keep1_ref[...] + from2_ref[1].astype(F32)).astype(BF16)
    to2_ref[...] = (keep2_ref[...] + from1_ref[1].astype(F32)).astype(BF16)
    sum_ref[:half] = own_ref[:half] + from1_ref[0].astype(F32)
    sum_ref[half:] = own_ref[half:] + from2_ref[0].astype(F32)


def slab_kernel(sum_ref, from1_ref, from2_ref, _, *outs):
    *outs, rows_ref = outs
    half = from1_ref.shape[0]
    rows_ref[:half] = sum_ref[:half] + from2_ref[...].astype(F32)
    rows_ref[half:] = sum_ref[half:] + from1_ref[...].astype(F32)
    for t, out in enumerate(outs):
        out[...] = rows_ref[position()[1] ^ t].astype(out.dtype)


def relay_kernel(x_ref, _, *outs):
    for i, out in enumerate(outs):
        out[...] = x_ref[i * out.shape[0] : (i + 1) * out.shape[0]]


def columns_of(ref, start, owned):
    high = ref.shape[0] - start
    chunk = [ref[start:, q * 128 : (q + 1) * 128] for q in range(owned // high)]
    return jnp.concatenate(chunk, axis=0)


def early_kernel(near, paired, got, far, mine_ref, other_ref, sum_ref):
    owned = mine_ref.shape[0]
    left = jnp.concatenate([near[:owned], paired[:owned]], axis=0)
    total = None
    for t, ref in enumerate((near, got, far)):
        rows = dot1(left, ref[:owned], NT)
        at = slice(t * owned, (t + 1) * owned)
        mine_ref[:, at] = rows[:owned]
        other_ref[:, at] = rows[owned:].astype(BF16)
        value = dot1(columns_of(ref, owned, owned), ref[:owned], TN)
        total = value if total is None else total + value
    sum_ref[...] = total


def late_kernel(count, near, paired, mine_early, other_early, sum_early, *refs):
    far = jnp.concatenate([ref[...] for ref in refs[:1]], axis=0)
    mine_ref, part_ref, other_ref, sum_ref = refs[1 + count :]
    owned, before = mine_early.shape
    half = owned // 2
    wide = mine_ref.shape[1]
    part = part_ref.shape[0]
    mine_ref[:, :before] = mine_early[...]
    left = jnp.concatenate([near[:owned], paired[:owned]], axis=0)
    rows = dot1(left, far[:owned], NT)
    mine_ref[:, before:] = rows[:owned]
    for i in range(2):
        at = slice(i * half, (i + 1) * half)
        other_ref[:half, i * wide : i * wide + before] = other_early[at]
        other_ref[:half, i * wide + before : (i + 1) * wide] = rows[owned:][at].astype(BF16)
    sum_ref[...] = sum_early[...] + dot1(columns_of(far, owned, owned), far[:owned], TN)
    part_ref[...] = sum_ref[pl.ds(pl.multiple_of(lax.rem(position()[3], 4) * part, part), part)]
    away = sum_ref[pl.ds(pl.multiple_of(lax.rem(position()[3] ^ 1, 4) * part, part), part)]
    other_ref[half : half + part], other_ref[half + part :] = halves(away)


def place_kernel(mine, came, *outs):
    *outs, rows_ref = outs
    owned, wide = mine.shape
    half = owned // 2
    for t in range(wide // owned):
        at = pl.multiple_of((position()[3] ^ (2 * t)) * owned, owned)
        rows_ref[:, pl.ds(at, owned)] = mine[:, t * owned : (t + 1) * owned]
        at = pl.multiple_of((position()[3] ^ (2 * t + 1)) * owned, owned)
        for i in range(2):
            part = came[:half, i * wide + t * owned : i * wide + (t + 1) * owned]
            rows_ref[i * half : (i + 1) * half, pl.ds(at, owned)] = part.astype(F32)
    height = owned // len(outs)
    for t, out in enumerate(outs):
        at = pl.multiple_of((position()[2] ^ t) * height, height)
        out[...] = rows_ref[pl.ds(at, height)].astype(out.dtype)


def last_kernel(scales, count, mine, came, *refs):
    parts, outs = refs[: 2 * count], refs[2 * count :]
    for i, scale in enumerate(scales):
        total = parts[i * count][...]
        for part in parts[i * count + 1 : (i + 1) * count]:
            total = total + part[...].astype(F32)
        outs[i][...] = total * scale
    slices, part, rank = outs[2].shape
    for k in range(slices):
        at = slice(k * rank, (k + 1) * rank)
        low = came[came.shape[0] - part :, at].astype(F32)
        high = came[came.shape[0] - 2 * part : came.shape[0] - part, at].astype(F32)
        outs[2][k] = mine[:, at] + (high + low)


def xor_permute(x, axis, bits):
    return lax.ppermute(x, axis, [(i, i ^ bits) for i in range(lax.axis_size(axis))])


def pick(x, index, axis):
    return lax.dynamic_index_in_dim(x, index, axis, keepdims=False)


def tiled_shards(tensor, factor_one, factor_two):
    slices, owned, width = tensor.shape
    count_ja = lax.axis_size("ja")
    count_ka = lax.axis_size("ka")
    count_z = count_ja // 2
    rank_one = factor_one.shape[1]
    part = factor_two.shape[1] // count_ja
    step = width // count_ja
    columns = slices * rank_one
    high = owned * 128 // columns
    norm_one = 1.0 / math.sqrt(owned * count_ja * slices * count_ka)
    norm_two = 1.0 / math.sqrt(slices * count_ka * rank_one)

    (away,) = call(
        away_kernel, "away", [((count_z, step, width), BF16)], [VMEM], tensor, vmem=4
    )
    near, far = call(
        core_kernel,
        "core",
        [((owned + high, columns), BF16)] * 2,
        [VMEM, VMEM, VMEM, ANY],
        tensor,
        factor_one,
        factor_two,
        away,
        vmem=4,
    )

    far2 = xor_permute(far, "ja", 4)
    got1 = xor_permute(near, "ja", 2)
    paired = xor_permute(near, "ja", 1)
    came = xor_permute(away, "ja", 1)

    shape = (count_z, step // count_ka, width)
    half = (count_z // 2, *shape[1:])
    own, keep1, keep2, to1, to2 = call(
        home_kernel,
        "home",
        [(shape, F32), (half, F32), (half, F32), ((2, *half), BF16), ((2, *half), BF16)],
        [VMEM, VMEM, ANY],
        tensor,
        came,
        paired,
        scratch=[pltpu.VMEM((count_z, step, min(256, width)), F32)],
        vmem=6,
    )
    from1 = xor_permute(to1, "ka", 1)
    from2 = xor_permute(to2, "ka", 2)
    total, to1, to2 = call(
        middle_kernel,
        "middle",
        [(shape, F32), (half, BF16), (half, BF16)],
        [VMEM] * 5 + [ANY] * 2,
        own,
        keep1,
        keep2,
        from1,
        from2,
        got1,
        far2,
    )
    from1 = xor_permute(to1, "ka", 1)
    from2 = xor_permute(to2, "ka", 2)
    far3 = call(relay_kernel, "relay", [(far.shape, BF16)], [VMEM, ANY], far2, total)
    far3 = [xor_permute(p, "ja", 2) for p in far3]
    begun = call(
        early_kernel,
        "two_early",
        [((owned, 3 * owned), F32), ((owned, 3 * owned), BF16), ((128, columns), F32)],
        [VMEM] * 4,
        near,
        paired,
        got1,
        far2,
    )
    sums = call(
        slab_kernel,
        "slab",
        [(shape[1:], F32 if t == 0 else BF16) for t in range(count_z)],
        [VMEM] * 3 + [ANY],
        total,
        from1,
        from2,
        begun[0],
        scratch=[pltpu.VMEM(shape, F32)],
    )
    sums = [p if t == 0 else xor_permute(p, "ja", 2 * t) for t, p in enumerate(sums)]

    waits = sums[:1]
    mine, mine_part, other = call(
        functools.partial(late_kernel, len(waits)),
        "two_late",
        [((owned, 4 * owned), F32), ((part, columns), F32), ((owned // 2 + 2 * part, columns), BF16)],
        [VMEM] * 6 + [ANY] * len(waits),
        near,
        paired,
        *begun,
        *far3,
        *waits,
        scratch=[pltpu.VMEM((128, columns), F32)],
    )
    other = xor_permute(other, "ja", 1)
    final = (owned // count_ka, count_ja * owned)
    rows = call(
        place_kernel,
        "two_place",
        [(final, F32 if t == 0 else BF16) for t in range(count_ka)],
        [VMEM] * 2,
        mine,
        other,
        scratch=[pltpu.VMEM((owned, count_ja * owned), F32)],
    )
    rows = [p if t == 0 else xor_permute(p, "ka", t) for t, p in enumerate(rows)]
    return call(
        functools.partial(last_kernel, (norm_one, norm_two), count_z),
        "last",
        [(shape[1:], F32), (final, F32), ((slices, part, rank_one), F32)],
        [VMEM] * (2 + count_z + count_ka),
        mine_part,
        other,
        *sums,
        *rows,
    )


def plain_shards(tensor, factor_one, factor_two):
    slices, owned, width = tensor.shape
    count_ja = lax.axis_size("ja")
    count_ka = lax.axis_size("ka")
    count_z = count_ja // 2
    rank_one = factor_one.shape[1]
    ja = lax.axis_index("ja")
    ka = lax.axis_index("ka")
    core_at, z = lax.rem(ja, 2), lax.div(ja, 2)
    step = width // count_ja
    x = halves(tensor.reshape(slices * owned, width))
    core = dot3(x, halves(factor_one), NN).astype(BF16).reshape(slices, owned, rank_one)
    u = core.transpose(1, 0, 2).reshape(owned, slices * rank_one)
    local = dot3(x, x, TN).reshape(count_z, 2, step, width)
    home = pick(local, core_at, 1)
    home = home + xor_permute(pick(local, 1 - core_at, 1).astype(BF16), "ja", 1).astype(F32)
    home = home.reshape(count_z, count_ka, step // count_ka, width)
    slab = pick(home, ka, 1)
    for t in range(1, count_ka):
        slab = slab + xor_permute(pick(home, ka ^ t, 1).astype(BF16), "ka", t).astype(F32)
    gram_one = pick(slab, z, 0)
    for t in range(1, count_z):
        gram_one = gram_one + xor_permute(pick(slab, z ^ t, 0).astype(BF16), "ja", 2 * t).astype(F32)
    gram_one = gram_one * (1.0 / math.sqrt(owned * count_ja * slices * count_ka))

    blocks = [u, xor_permute(u, "ja", 1)]
    for t in range(1, count_z):
        block = xor_permute(u, "ja", 2 * t)
        blocks += [block, xor_permute(block, "ja", 1)]
    places = jnp.arange(count_ja) ^ ja
    gathered = jnp.take(jnp.stack(blocks), places, axis=0).reshape(count_ja * owned, -1)
    rows = dot1(u, gathered, NT).reshape(count_ka, owned // count_ka, count_ja * owned)
    gram_two = pick(rows, ka, 0)
    for t in range(1, count_ka):
        gram_two = gram_two + xor_permute(pick(rows, ka ^ t, 0).astype(BF16), "ka", t).astype(F32)
    gram_two = gram_two * (1.0 / math.sqrt(slices * count_ka * rank_one))

    cut = factor_two.reshape(owned, count_ja, -1)
    two = [pick(cut, ja, 1)]
    two += [xor_permute(pick(cut, ja ^ b, 1), "ja", b) for b in range(1, count_ja)]
    two = jnp.take(jnp.stack(two), places, axis=0).reshape(count_ja * owned, -1)
    reduced = dot1(two, gathered, TN).reshape(-1, slices, rank_one).transpose(1, 0, 2)
    return (gram_one, gram_two, reduced)


def shards(tensor, factor_one, factor_two):
    slices, owned, width = tensor.shape
    count_ja = lax.axis_size("ja")
    count_ka = lax.axis_size("ka")
    step = width // count_ja
    columns = slices * factor_one.shape[1]
    tiled = count_ja == 8 and count_ka == 4 and factor_two.shape[1] == 256
    tiled = tiled and step % 128 == 0 and owned % 128 == 0
    tiled = tiled and step % (16 * count_ka) == 0 and owned % (16 * count_ka) == 0
    tiled = tiled and owned * 128 % (16 * columns) == 0 and columns % 128 == 0
    tiled = tiled and columns == 8 * owned and owned == 128
    return (tiled_shards if tiled else plain_shards)(tensor, factor_one, factor_two)


def solution(mesh):
    in_specs = (P("ka", "ja", None), P(), P("ja", None))
    out_specs = (P(("ja", "ka"), None), P(("ja", "ka"), None), P("ka", "ja", None))
    return jax.shard_map(shards, mesh=mesh, in_specs=in_specs, out_specs=out_specs, check_vma=False)
```

```python
import functools
import math

import jax
import jax.numpy as jnp
from jax import lax
from jax.experimental import pallas as pl
from jax.experimental.pallas import tpu as pltpu
from jax.sharding import PartitionSpec as P

F32 = jnp.float32
BF16 = jnp.bfloat16
NN = (((1,), (0,)), ((), ()))
NT = (((1,), (1,)), ((), ()))
TN = (((0,), (0,)), ((), ()))
VMEM = pl.BlockSpec(memory_space=pltpu.VMEM)
ANY = pl.BlockSpec(memory_space=pl.ANY)


def halves(x):
    high = x.astype(BF16)
    return high, (x - high.astype(F32)).astype(BF16)


def dot1(a, b, dims):
    return lax.dot_general(a, b, dims, preferred_element_type=F32)


def dot3(a, b, dims):
    return dot1(a[0], b[0], dims) + (dot1(a[0], b[1], dims) + dot1(a[1], b[0], dims))


def call(kernel, name, outs, in_specs, *args, scratch=(), vmem=4, flops=0):
    return pl.pallas_call(
        kernel,
        out_shape=[jax.ShapeDtypeStruct(s, d) for s, d in outs],
        in_specs=in_specs,
        out_specs=[VMEM] * len(outs),
        scratch_shapes=list(scratch),
        compiler_params=pltpu.CompilerParams(vmem_limit_bytes=vmem * 1024 * 1024),
        cost_estimate=pl.CostEstimate(flops=flops, bytes_accessed=0, transcendentals=0),
        name=name,
    )(*args)


def position():
    ja = lax.axis_index("ja")
    return lax.rem(ja, 2), lax.div(ja, 2), lax.axis_index("ka"), ja


def gram_rows(core, x_ref, groups, step, keep):
    slices, owned, width = x_ref.shape
    at = [pl.multiple_of((2 * g + core) * step, step) for g in range(groups)]
    left = [x_ref[:, :, pl.ds(a, step)].reshape(slices * owned, step) for a in at]
    left = halves(jnp.concatenate(left, axis=1).T)
    wide = min(256, width)
    for n in range(0, width, wide):
        right = halves(x_ref[:, :, n : n + wide].reshape(slices * owned, wide))
        keep(slice(n, n + wide), dot3(left, right, NN).reshape(groups, step, wide))


def away_kernel(x_ref, away_ref):
    groups, step, _ = away_ref.shape

    def keep(at, rows):
        away_ref[:, :, at] = rows.astype(BF16)

    gram_rows(1 - position()[0], x_ref, groups, step, keep)


def core_kernel(x_ref, f_ref, two_ref, _, near_ref, far_ref):
    slices, owned, _ = x_ref.shape
    rank = f_ref.shape[1]
    high = far_ref.shape[0] - owned
    other = 1 - lax.div(position()[1], 2)
    chunk = two_ref[:, pl.ds(pl.multiple_of(other * 128, 128), 128)]
    for q in range(owned // high):
        far_ref[owned:, q * 128 : (q + 1) * 128] = chunk[q * high : (q + 1) * high]
    f = halves(f_ref[...])
    for k in range(slices):
        core = dot3(halves(x_ref[k]), f, NN).astype(BF16)
        at = slice(k * rank, (k + 1) * rank)
        near_ref[:owned, at] = core
        far_ref[:owned, at] = core


def home_kernel(x_ref, came_ref, _, own_ref, keep1_ref, keep2_ref, to1_ref, to2_ref, rows_ref):
    groups, step, _ = came_ref.shape
    block = own_ref.shape[1]
    lower, upper = slice(0, groups // 2), slice(groups // 2, groups)

    def keep(at, rows):
        rows_ref[...] = rows + came_ref[:, :, at].astype(F32)

        def part(chips, t):
            return rows_ref[chips, pl.ds(pl.multiple_of((position()[2] ^ t) * block, block), block)]

        own_ref[:, :, at] = part(slice(0, groups), 0)
        keep1_ref[:, :, at] = part(upper, 1)
        keep2_ref[:, :, at] = part(lower, 2)
        for i, t in enumerate((1, 3)):
            to1_ref[i, :, :, at] = part(lower, t).astype(BF16)
        for i, t in enumerate((2, 3)):
            to2_ref[i, :, :, at] = part(upper, t).astype(BF16)

    gram_rows(position()[0], x_ref, groups, step, keep)


def middle_kernel(own_ref, keep1_ref, keep2_ref, from1_ref, from2_ref, sum_ref, to1_ref, to2_ref):
    half = from1_ref.shape[1]
    count = half * from1_ref.shape[2]
    for out, keep, came in ((to1_ref, keep1_ref, from2_ref), (to2_ref, keep2_ref, from1_ref)):
        out[:count] = (keep[...] + came[1].astype(F32)).astype(BF16).reshape(count, out.shape[1])
        out[count:] = jnp.zeros((out.shape[0] - count, out.shape[1]), BF16)
    sum_ref[:half] = own_ref[:half] + from1_ref[0].astype(F32)
    sum_ref[half:] = own_ref[half:] + from2_ref[0].astype(F32)


def slab_kernel(sum_ref, from1_ref, from2_ref, mine_ref, came_ref, *refs):
    *outs, part_ref, rows_ref = refs[1:]
    half, height = sum_ref.shape[0] // 2, sum_ref.shape[1]
    count = half * height
    part = part_ref.shape[0]
    came = [ref[:count].astype(F32).reshape(half, height, ref.shape[1]) for ref in (from1_ref, from2_ref)]
    rows_ref[:half] = sum_ref[:half] + came[1]
    rows_ref[half:] = sum_ref[half:] + came[0]
    for t, out in enumerate(outs):
        out[:height] = rows_ref[position()[1] ^ t].astype(out.dtype)
    part_ref[...] = mine_ref[:part] + came_ref[:part].astype(F32)
    outs[1][height:] = (mine_ref[part:] + came_ref[part:].astype(F32)).astype(BF16)


def near_kernel(u, paired, got, mine_ref, other_ref):
    owned = mine_ref.shape[0]
    left = jnp.concatenate([u[:owned], paired[:owned]], axis=0)
    for t, block in enumerate((u, got)):
        rows = dot1(left, block[:owned], NT)
        at = slice(t * owned, (t + 1) * owned)
        mine_ref[:, at] = rows[:owned]
        other_ref[:, at] = rows[owned:].astype(BF16)


def cross_kernel(u, paired, got, got_paired, far, _, mine_ref, other_ref, send_ref):
    owned = mine_ref.shape[0]
    left = [ref[:owned] for ref in (u, paired, got, got_paired)]
    rows = dot1(jnp.concatenate(left, axis=0), far[:owned], NT)
    mine_ref[...] = rows[:owned]
    other_ref[...] = rows[owned : 2 * owned].astype(BF16)
    send_ref[...] = rows[2 * owned :].astype(BF16)


def merge_kernel(mine_near, other_near, mine_far, other_far, came, _, mine_ref, other_ref):
    owned, before = mine_near.shape
    half, wide = owned // 2, mine_ref.shape[1]
    mine_ref[:, :before] = mine_near[...]
    mine_ref[:, before : before + owned] = mine_far[...]
    mine_ref[:, before + owned :] = came[:owned].astype(F32)
    for i in range(2):
        at, start = slice(i * half, (i + 1) * half), i * wide
        other_ref[:, start : start + before] = other_near[at]
        other_ref[:, start + before : start + before + owned] = other_far[at]
        other_ref[:, start + before + owned : start + wide] = came[owned + i * half : owned + (i + 1) * half]


def parts_kernel(u, far, two_ref, _, mine_ref, other_ref, sum_ref):
    owned = two_ref.shape[0]
    part = mine_ref.shape[0] // 2
    high = far.shape[0] - owned
    _, z, _, ja = position()
    own = two_ref[:, pl.ds(pl.multiple_of(lax.div(z, 2) * 128, 128), 128)]
    chunk = [far[owned:, q * 128 : (q + 1) * 128] for q in range(owned // high)]
    sum_ref[...] = dot1(own, u[:owned], TN) + dot1(jnp.concatenate(chunk, axis=0), far[:owned], TN)
    for t in range(4):
        start = pl.multiple_of(lax.rem(ja ^ t, 4) * part, part)
        out = (mine_ref, other_ref)[t % 2]
        out[t // 2 * part : (t // 2 + 1) * part] = sum_ref[pl.ds(start, part)].astype(out.dtype)


def place_kernel(mine, came, *outs):
    *outs, rows_ref = outs
    owned, wide = mine.shape
    half = owned // 2
    for t in range(wide // owned):
        at = pl.multiple_of((position()[3] ^ (2 * t)) * owned, owned)
        rows_ref[:, pl.ds(at, owned)] = mine[:, t * owned : (t + 1) * owned]
        at = pl.multiple_of((position()[3] ^ (2 * t + 1)) * owned, owned)
        for i in range(2):
            part = came[:, i * wide + t * owned : i * wide + (t + 1) * owned]
            rows_ref[i * half : (i + 1) * half, pl.ds(at, owned)] = part.astype(F32)
    height = owned // len(outs)
    for t, out in enumerate(outs):
        at = pl.multiple_of((position()[2] ^ t) * height, height)
        out[...] = rows_ref[pl.ds(at, height)].astype(out.dtype)


def last_kernel(scales, count, mine, *refs):
    parts, outs = refs[: 2 * count], refs[2 * count :]
    for i, scale in enumerate(scales):
        total = parts[i * count][...]
        for part in parts[i * count + 1 : (i + 1) * count]:
            total = total + part[: total.shape[0]].astype(F32)
        outs[i][...] = total * scale
    slices, _, rank = outs[2].shape
    for k in range(slices):
        at = slice(k * rank, (k + 1) * rank)
        outs[2][k] = mine[:, at] + parts[1][parts[0].shape[0] :, at].astype(F32)


def xor_permute(x, axis, bits):
    return lax.ppermute(x, axis, [(i, i ^ bits) for i in range(lax.axis_size(axis))])


def pick(x, index, axis):
    return lax.dynamic_index_in_dim(x, index, axis, keepdims=False)


def tiled_shards(tensor, factor_one, factor_two):
    slices, owned, width = tensor.shape
    count_ja = lax.axis_size("ja")
    count_ka = lax.axis_size("ka")
    count_z = count_ja // 2
    rank_one = factor_one.shape[1]
    part = factor_two.shape[1] // count_ja
    step = width // count_ja
    columns = slices * rank_one
    high = owned * 128 // columns
    norm_one = 1.0 / math.sqrt(owned * count_ja * slices * count_ka)
    norm_two = 1.0 / math.sqrt(slices * count_ka * rank_one)

    (away,) = call(
        away_kernel, "away", [((count_z, step, width), BF16)], [VMEM], tensor, vmem=4
    )
    near, far = call(
        core_kernel,
        "core",
        [((owned, columns), BF16), ((owned + high, columns), BF16)],
        [VMEM, VMEM, VMEM, ANY],
        tensor,
        factor_one,
        factor_two,
        away,
        vmem=4,
    )

    far2 = xor_permute(far, "ja", 4)
    got1 = xor_permute(near, "ja", 2)
    paired = xor_permute(near, "ja", 1)
    came = xor_permute(away, "ja", 1)

    shape = (count_z, step // count_ka, width)
    half = (count_z // 2, *shape[1:])
    own, keep1, keep2, to1, to2 = call(
        home_kernel,
        "home",
        [(shape, F32), (half, F32), (half, F32), ((2, *half), BF16), ((2, *half), BF16)],
        [VMEM, VMEM, ANY],
        tensor,
        came,
        paired,
        scratch=[pltpu.VMEM((count_z, step, min(256, width)), F32)],
        vmem=6,
    )
    from1 = xor_permute(to1, "ka", 1)
    from2 = xor_permute(to2, "ka", 2)
    total, to1, to2 = call(
        middle_kernel,
        "middle",
        [(shape, F32)] + [((half[0] * half[1] + 16, width), BF16)] * 2,
        [VMEM] * 5,
        own,
        keep1,
        keep2,
        from1,
        from2,
    )
    from1 = xor_permute(to1, "ka", 1)
    from2 = xor_permute(to2, "ka", 2)
    got_paired = xor_permute(got1, "ja", 1)
    first = call(
        near_kernel,
        "two_near",
        [((owned, 2 * owned), F32), ((owned, 2 * owned), BF16)],
        [VMEM] * 3,
        near,
        paired,
        got1,
    )
    *second, send = call(
        cross_kernel,
        "two_cross",
        [((owned, owned), F32), ((owned, owned), BF16), ((2 * owned, owned), BF16)],
        [VMEM] * 5 + [ANY],
        near,
        paired,
        got1,
        got_paired,
        far2,
        total,
    )
    crossed = xor_permute(send, "ja", 2)
    mine_part, other_part = call(
        parts_kernel,
        "parts",
        [((2 * part, columns), F32), ((2 * part, columns), BF16)],
        [VMEM] * 3 + [ANY],
        near,
        far2,
        factor_two,
        send,
        scratch=[pltpu.VMEM((128, columns), F32)],
    )
    height = step // count_ka
    *sums, mine_part = call(
        slab_kernel,
        "slab",
        [
            ((height + (part if t == 1 else 0), width), F32 if t == 0 else BF16)
            for t in range(count_z)
        ]
        + [((part, columns), F32)],
        [VMEM] * 5 + [ANY],
        total,
        from1,
        from2,
        mine_part,
        xor_permute(other_part, "ja", 1),
        crossed,
        scratch=[pltpu.VMEM(shape, F32)],
    )
    sums = list(sums)
    for t in reversed(range(1, count_z)):
        sums[t] = xor_permute(sums[t], "ja", 2 * t)
    mine, other = call(
        merge_kernel,
        "two_merge",
        [((owned, 4 * owned), F32), ((owned // 2, 8 * owned), BF16)],
        [VMEM] * 5 + [ANY],
        *first,
        *second,
        crossed,
        sums[0],
    )
    other = xor_permute(other, "ja", 1)
    final = (owned // count_ka, count_ja * owned)
    rows = call(
        place_kernel,
        "two_place",
        [(final, F32 if t == 0 else BF16) for t in range(count_ka)],
        [VMEM] * 2,
        mine,
        other,
        scratch=[pltpu.VMEM((owned, count_ja * owned), F32)],
    )
    rows = list(rows)
    for t in reversed(range(1, count_ka)):
        rows[t] = xor_permute(rows[t], "ka", t)
    return call(
        functools.partial(last_kernel, (norm_one, norm_two), count_z),
        "last",
        [((height, width), F32), (final, F32), ((slices, part, rank_one), F32)],
        [VMEM] * (1 + count_z + count_ka),
        mine_part,
        *sums,
        *rows,
    )


def plain_shards(tensor, factor_one, factor_two):
    slices, owned, width = tensor.shape
    count_ja = lax.axis_size("ja")
    count_ka = lax.axis_size("ka")
    count_z = count_ja // 2
    rank_one = factor_one.shape[1]
    ja = lax.axis_index("ja")
    ka = lax.axis_index("ka")
    core_at, z = lax.rem(ja, 2), lax.div(ja, 2)
    step = width // count_ja
    x = halves(tensor.reshape(slices * owned, width))
    core = dot3(x, halves(factor_one), NN).astype(BF16).reshape(slices, owned, rank_one)
    u = core.transpose(1, 0, 2).reshape(owned, slices * rank_one)
    local = dot3(x, x, TN).reshape(count_z, 2, step, width)
    home = pick(local, core_at, 1)
    home = home + xor_permute(pick(local, 1 - core_at, 1).astype(BF16), "ja", 1).astype(F32)
    home = home.reshape(count_z, count_ka, step // count_ka, width)
    slab = pick(home, ka, 1)
    for t in range(1, count_ka):
        slab = slab + xor_permute(pick(home, ka ^ t, 1).astype(BF16), "ka", t).astype(F32)
    gram_one = pick(slab, z, 0)
    for t in range(1, count_z):
        gram_one = gram_one + xor_permute(pick(slab, z ^ t, 0).astype(BF16), "ja", 2 * t).astype(F32)
    gram_one = gram_one * (1.0 / math.sqrt(owned * count_ja * slices * count_ka))

    blocks = [u, xor_permute(u, "ja", 1)]
    for t in range(1, count_z):
        block = xor_permute(u, "ja", 2 * t)
        blocks += [block, xor_permute(block, "ja", 1)]
    places = jnp.arange(count_ja) ^ ja
    gathered = jnp.take(jnp.stack(blocks), places, axis=0).reshape(count_ja * owned, -1)
    rows = dot1(u, gathered, NT).reshape(count_ka, owned // count_ka, count_ja * owned)
    gram_two = pick(rows, ka, 0)
    for t in range(1, count_ka):
        gram_two = gram_two + xor_permute(pick(rows, ka ^ t, 0).astype(BF16), "ka", t).astype(F32)
    gram_two = gram_two * (1.0 / math.sqrt(slices * count_ka * rank_one))

    cut = factor_two.reshape(owned, count_ja, -1)
    two = [pick(cut, ja, 1)]
    two += [xor_permute(pick(cut, ja ^ b, 1), "ja", b) for b in range(1, count_ja)]
    two = jnp.take(jnp.stack(two), places, axis=0).reshape(count_ja * owned, -1)
    reduced = dot1(two, gathered, TN).reshape(-1, slices, rank_one).transpose(1, 0, 2)
    return (gram_one, gram_two, reduced)


def shards(tensor, factor_one, factor_two):
    slices, owned, width = tensor.shape
    count_ja = lax.axis_size("ja")
    count_ka = lax.axis_size("ka")
    step = width // count_ja
    columns = slices * factor_one.shape[1]
    tiled = count_ja == 8 and count_ka == 4 and factor_two.shape[1] == 256
    tiled = tiled and step % 128 == 0 and owned % 128 == 0
    tiled = tiled and step % (16 * count_ka) == 0 and owned % (16 * count_ka) == 0
    tiled = tiled and owned * 128 % (16 * columns) == 0 and columns % 128 == 0
    tiled = tiled and columns == 8 * owned and owned == 128
    return (tiled_shards if tiled else plain_shards)(tensor, factor_one, factor_two)


def solution(mesh):
    in_specs = (P("ka", "ja", None), P(), P("ja", None))
    out_specs = (P(("ja", "ka"), None), P(("ja", "ka"), None), P("ka", "ja", None))
    return jax.shard_map(shards, mesh=mesh, in_specs=in_specs, out_specs=out_specs, check_vma=False)
```

```python
import functools
import math

import jax
import jax.numpy as jnp
from jax import lax
from jax.experimental import pallas as pl
from jax.experimental.pallas import tpu as pltpu
from jax.sharding import PartitionSpec as P

F32 = jnp.float32
BF16 = jnp.bfloat16
NN = (((1,), (0,)), ((), ()))
NT = (((1,), (1,)), ((), ()))
TN = (((0,), (0,)), ((), ()))
VMEM = pl.BlockSpec(memory_space=pltpu.VMEM)
ANY = pl.BlockSpec(memory_space=pl.ANY)


def halves(x):
    high = x.astype(BF16)
    return high, (x - high.astype(F32)).astype(BF16)


def dot1(a, b, dims):
    return lax.dot_general(a, b, dims, preferred_element_type=F32)


def dot3(a, b, dims):
    return dot1(a[0], b[0], dims) + (dot1(a[0], b[1], dims) + dot1(a[1], b[0], dims))


def call(kernel, name, outs, in_specs, *args, scratch=(), vmem=4, flops=0):
    return pl.pallas_call(
        kernel,
        out_shape=[jax.ShapeDtypeStruct(s, d) for s, d in outs],
        in_specs=in_specs,
        out_specs=[VMEM] * len(outs),
        scratch_shapes=list(scratch),
        compiler_params=pltpu.CompilerParams(vmem_limit_bytes=vmem * 1024 * 1024),
        cost_estimate=pl.CostEstimate(flops=flops, bytes_accessed=0, transcendentals=0),
        name=name,
    )(*args)


def position():
    ja = lax.axis_index("ja")
    return lax.rem(ja, 2), lax.div(ja, 2), lax.axis_index("ka"), ja


def gram_rows(core, x_ref, groups, step, keep):
    slices, owned, width = x_ref.shape
    at = [pl.multiple_of((2 * g + core) * step, step) for g in range(groups)]
    left = [x_ref[:, :, pl.ds(a, step)].reshape(slices * owned, step) for a in at]
    left = halves(jnp.concatenate(left, axis=1).T)
    wide = min(256, width)
    for n in range(0, width, wide):
        right = halves(x_ref[:, :, n : n + wide].reshape(slices * owned, wide))
        keep(slice(n, n + wide), dot3(left, right, NN).reshape(groups, step, wide))


def away_kernel(x_ref, away_ref):
    groups, step, _ = away_ref.shape

    def keep(at, rows):
        away_ref[:, :, at] = rows.astype(BF16)

    gram_rows(1 - position()[0], x_ref, groups, step, keep)


def core_kernel(x_ref, f_ref, two_ref, _, near_ref, far_ref):
    slices, owned, _ = x_ref.shape
    rank = f_ref.shape[1]
    high = far_ref.shape[0] - owned
    other = 1 - lax.div(position()[1], 2)
    chunk = two_ref[:, pl.ds(pl.multiple_of(other * 128, 128), 128)]
    for q in range(owned // high):
        far_ref[owned:, q * 128 : (q + 1) * 128] = chunk[q * high : (q + 1) * high]
    f = halves(f_ref[...])
    for k in range(slices):
        core = dot3(halves(x_ref[k]), f, NN).astype(BF16)
        at = slice(k * rank, (k + 1) * rank)
        near_ref[:owned, at] = core
        far_ref[:owned, at] = core


def home_kernel(x_ref, came_ref, _, own_ref, keep1_ref, keep2_ref, to1_ref, to2_ref, rows_ref):
    groups, step, _ = came_ref.shape
    block = own_ref.shape[1]
    lower, upper = slice(0, groups // 2), slice(groups // 2, groups)

    def keep(at, rows):
        rows_ref[...] = rows + came_ref[:, :, at].astype(F32)

        def part(chips, t):
            return rows_ref[chips, pl.ds(pl.multiple_of((position()[2] ^ t) * block, block), block)]

        own_ref[:, :, at] = part(slice(0, groups), 0)
        keep1_ref[:, :, at] = part(upper, 1)
        keep2_ref[:, :, at] = part(lower, 2)
        for i, t in enumerate((1, 3)):
            to1_ref[i, :, :, at] = part(lower, t).astype(BF16)
        for i, t in enumerate((2, 3)):
            to2_ref[i, :, :, at] = part(upper, t).astype(BF16)

    gram_rows(position()[0], x_ref, groups, step, keep)


def middle_kernel(own_ref, keep1_ref, keep2_ref, from1_ref, from2_ref, sum_ref, to1_ref, to2_ref):
    half = from1_ref.shape[1]
    count = half * from1_ref.shape[2]
    for out, keep, came in ((to1_ref, keep1_ref, from2_ref), (to2_ref, keep2_ref, from1_ref)):
        out[:count] = (keep[...] + came[1].astype(F32)).astype(BF16).reshape(count, out.shape[1])
        out[count:] = jnp.zeros((out.shape[0] - count, out.shape[1]), BF16)
    sum_ref[:half] = own_ref[:half] + from1_ref[0].astype(F32)
    sum_ref[half:] = own_ref[half:] + from2_ref[0].astype(F32)


def slab_kernel(sum_ref, from1_ref, from2_ref, mine_ref, came_ref, *refs):
    *outs, part_ref, rows_ref = refs[1:]
    half, height = sum_ref.shape[0] // 2, sum_ref.shape[1]
    count = half * height
    part = part_ref.shape[0]
    came = [ref[:count].astype(F32).reshape(half, height, ref.shape[1]) for ref in (from1_ref, from2_ref)]
    rows_ref[:half] = sum_ref[:half] + came[1]
    rows_ref[half:] = sum_ref[half:] + came[0]
    for t, out in enumerate(outs):
        out[:height] = rows_ref[position()[1] ^ t].astype(out.dtype)
    part_ref[...] = mine_ref[:part] + came_ref[:part].astype(F32)
    high, low = halves(mine_ref[part:] + came_ref[part:].astype(F32))
    outs[1][height : height + part] = high
    outs[1][height + part :] = low


def near_kernel(u, paired, got, mine_ref, other_ref):
    owned = mine_ref.shape[0]
    left = jnp.concatenate([u[:owned], paired[:owned]], axis=0)
    for t, block in enumerate((u, got)):
        rows = dot1(left, block[:owned], NT)
        at = slice(t * owned, (t + 1) * owned)
        mine_ref[:, at] = rows[:owned]
        other_ref[:, at] = rows[owned:].astype(BF16)


def cross_kernel(u, paired, got, got_paired, far, _, mine_ref, other_ref, send_ref):
    owned = mine_ref.shape[0]
    left = [ref[:owned] for ref in (u, paired, got, got_paired)]
    rows = dot1(jnp.concatenate(left, axis=0), far[:owned], NT)
    mine_ref[...] = rows[:owned]
    other_ref[...] = rows[owned : 2 * owned].astype(BF16)
    send_ref[...] = rows[2 * owned :].astype(BF16)


def merge_kernel(mine_near, other_near, mine_far, other_far, came, _, mine_ref, other_ref):
    owned, before = mine_near.shape
    half, wide = owned // 2, mine_ref.shape[1]
    mine_ref[:, :before] = mine_near[...]
    mine_ref[:, before : before + owned] = mine_far[...]
    mine_ref[:, before + owned :] = came[:owned].astype(F32)
    for i in range(2):
        at, start = slice(i * half, (i + 1) * half), i * wide
        other_ref[:, start : start + before] = other_near[at]
        other_ref[:, start + before : start + before + owned] = other_far[at]
        other_ref[:, start + before + owned : start + wide] = came[owned + i * half : owned + (i + 1) * half]


def parts_kernel(u, far, two_ref, _, mine_ref, other_ref, sum_ref):
    owned = two_ref.shape[0]
    part = mine_ref.shape[0] // 2
    high = far.shape[0] - owned
    _, z, _, ja = position()
    own = two_ref[:, pl.ds(pl.multiple_of(lax.div(z, 2) * 128, 128), 128)]
    chunk = [far[owned:, q * 128 : (q + 1) * 128] for q in range(owned // high)]
    sum_ref[...] = dot1(own, u[:owned], TN) + dot1(jnp.concatenate(chunk, axis=0), far[:owned], TN)
    for t in range(4):
        start = pl.multiple_of(lax.rem(ja ^ t, 4) * part, part)
        out = (mine_ref, other_ref)[t % 2]
        out[t // 2 * part : (t // 2 + 1) * part] = sum_ref[pl.ds(start, part)].astype(out.dtype)


def place_kernel(mine, came, *outs):
    *outs, rows_ref = outs
    owned, wide = mine.shape
    half = owned // 2
    for t in range(wide // owned):
        at = pl.multiple_of((position()[3] ^ (2 * t)) * owned, owned)
        rows_ref[:, pl.ds(at, owned)] = mine[:, t * owned : (t + 1) * owned]
        at = pl.multiple_of((position()[3] ^ (2 * t + 1)) * owned, owned)
        for i in range(2):
            part = came[:, i * wide + t * owned : i * wide + (t + 1) * owned]
            rows_ref[i * half : (i + 1) * half, pl.ds(at, owned)] = part.astype(F32)
    height = owned // len(outs)
    for t, out in enumerate(outs):
        at = pl.multiple_of((position()[2] ^ t) * height, height)
        out[...] = rows_ref[pl.ds(at, height)].astype(out.dtype)


def last_kernel(scales, count, mine, *refs):
    parts, outs = refs[: 2 * count], refs[2 * count :]
    for i, scale in enumerate(scales):
        total = parts[i * count][...]
        for part in parts[i * count + 1 : (i + 1) * count]:
            total = total + part[: total.shape[0]].astype(F32)
        outs[i][...] = total * scale
    slices, part, rank = outs[2].shape
    height = parts[0].shape[0]
    for k in range(slices):
        at = slice(k * rank, (k + 1) * rank)
        came = parts[1][height : height + part, at].astype(F32) + parts[1][height + part :, at].astype(F32)
        outs[2][k] = mine[:, at] + came


def xor_permute(x, axis, bits):
    return lax.ppermute(x, axis, [(i, i ^ bits) for i in range(lax.axis_size(axis))])


def pick(x, index, axis):
    return lax.dynamic_index_in_dim(x, index, axis, keepdims=False)


def tiled_shards(tensor, factor_one, factor_two):
    slices, owned, width = tensor.shape
    count_ja = lax.axis_size("ja")
    count_ka = lax.axis_size("ka")
    count_z = count_ja // 2
    rank_one = factor_one.shape[1]
    part = factor_two.shape[1] // count_ja
    step = width // count_ja
    columns = slices * rank_one
    high = owned * 128 // columns
    norm_one = 1.0 / math.sqrt(owned * count_ja * slices * count_ka)
    norm_two = 1.0 / math.sqrt(slices * count_ka * rank_one)

    (away,) = call(
        away_kernel, "away", [((count_z, step, width), BF16)], [VMEM], tensor, vmem=4
    )
    near, far = call(
        core_kernel,
        "core",
        [((owned, columns), BF16), ((owned + high, columns), BF16)],
        [VMEM, VMEM, VMEM, ANY],
        tensor,
        factor_one,
        factor_two,
        away,
        vmem=4,
    )

    far2 = xor_permute(far, "ja", 4)
    got1 = xor_permute(near, "ja", 2)
    paired = xor_permute(near, "ja", 1)
    came = xor_permute(away, "ja", 1)

    shape = (count_z, step // count_ka, width)
    half = (count_z // 2, *shape[1:])
    own, keep1, keep2, to1, to2 = call(
        home_kernel,
        "home",
        [(shape, F32), (half, F32), (half, F32), ((2, *half), BF16), ((2, *half), BF16)],
        [VMEM, VMEM, ANY],
        tensor,
        came,
        paired,
        scratch=[pltpu.VMEM((count_z, step, min(256, width)), F32)],
        vmem=6,
    )
    from1 = xor_permute(to1, "ka", 1)
    from2 = xor_permute(to2, "ka", 2)
    total, to1, to2 = call(
        middle_kernel,
        "middle",
        [(shape, F32)] + [((half[0] * half[1] + 16, width), BF16)] * 2,
        [VMEM] * 5,
        own,
        keep1,
        keep2,
        from1,
        from2,
    )
    from1 = xor_permute(to1, "ka", 1)
    from2 = xor_permute(to2, "ka", 2)
    got_paired = xor_permute(got1, "ja", 1)
    first = call(
        near_kernel,
        "two_near",
        [((owned, 2 * owned), F32), ((owned, 2 * owned), BF16)],
        [VMEM] * 3,
        near,
        paired,
        got1,
    )
    *second, send = call(
        cross_kernel,
        "two_cross",
        [((owned, owned), F32), ((owned, owned), BF16), ((2 * owned, owned), BF16)],
        [VMEM] * 5 + [ANY],
        near,
        paired,
        got1,
        got_paired,
        far2,
        total,
    )
    crossed = xor_permute(send, "ja", 2)
    mine_part, other_part = call(
        parts_kernel,
        "parts",
        [((2 * part, columns), F32), ((2 * part, columns), BF16)],
        [VMEM] * 3 + [ANY],
        near,
        far2,
        factor_two,
        send,
        scratch=[pltpu.VMEM((128, columns), F32)],
    )
    height = step // count_ka
    *sums, mine_part = call(
        slab_kernel,
        "slab",
        [
            ((height + (2 * part if t == 1 else 0), width), F32 if t == 0 else BF16)
            for t in range(count_z)
        ]
        + [((part, columns), F32)],
        [VMEM] * 5 + [ANY],
        total,
        from1,
        from2,
        mine_part,
        xor_permute(other_part, "ja", 1),
        crossed,
        scratch=[pltpu.VMEM(shape, F32)],
    )
    sums = list(sums)
    for t in reversed(range(1, count_z)):
        sums[t] = xor_permute(sums[t], "ja", 2 * t)
    mine, other = call(
        merge_kernel,
        "two_merge",
        [((owned, 4 * owned), F32), ((owned // 2, 8 * owned), BF16)],
        [VMEM] * 5 + [ANY],
        *first,
        *second,
        crossed,
        sums[0],
    )
    other = xor_permute(other, "ja", 1)
    final = (owned // count_ka, count_ja * owned)
    rows = call(
        place_kernel,
        "two_place",
        [(final, F32 if t == 0 else BF16) for t in range(count_ka)],
        [VMEM] * 2,
        mine,
        other,
        scratch=[pltpu.VMEM((owned, count_ja * owned), F32)],
    )
    rows = list(rows)
    for t in range(1, count_ka):
        rows[t] = xor_permute(rows[t], "ka", t)
    return call(
        functools.partial(last_kernel, (norm_one, norm_two), count_z),
        "last",
        [((height, width), F32), (final, F32), ((slices, part, rank_one), F32)],
        [VMEM] * (1 + count_z + count_ka),
        mine_part,
        *sums,
        *rows,
    )


def plain_shards(tensor, factor_one, factor_two):
    slices, owned, width = tensor.shape
    count_ja = lax.axis_size("ja")
    count_ka = lax.axis_size("ka")
    count_z = count_ja // 2
    rank_one = factor_one.shape[1]
    ja = lax.axis_index("ja")
    ka = lax.axis_index("ka")
    core_at, z = lax.rem(ja, 2), lax.div(ja, 2)
    step = width // count_ja
    x = halves(tensor.reshape(slices * owned, width))
    core = dot3(x, halves(factor_one), NN).astype(BF16).reshape(slices, owned, rank_one)
    u = core.transpose(1, 0, 2).reshape(owned, slices * rank_one)
    local = dot3(x, x, TN).reshape(count_z, 2, step, width)
    home = pick(local, core_at, 1)
    home = home + xor_permute(pick(local, 1 - core_at, 1).astype(BF16), "ja", 1).astype(F32)
    home = home.reshape(count_z, count_ka, step // count_ka, width)
    slab = pick(home, ka, 1)
    for t in range(1, count_ka):
        slab = slab + xor_permute(pick(home, ka ^ t, 1).astype(BF16), "ka", t).astype(F32)
    gram_one = pick(slab, z, 0)
    for t in range(1, count_z):
        gram_one = gram_one + xor_permute(pick(slab, z ^ t, 0).astype(BF16), "ja", 2 * t).astype(F32)
    gram_one = gram_one * (1.0 / math.sqrt(owned * count_ja * slices * count_ka))

    blocks = [u, xor_permute(u, "ja", 1)]
    for t in range(1, count_z):
        block = xor_permute(u, "ja", 2 * t)
        blocks += [block, xor_permute(block, "ja", 1)]
    places = jnp.arange(count_ja) ^ ja
    gathered = jnp.take(jnp.stack(blocks), places, axis=0).reshape(count_ja * owned, -1)
    rows = dot1(u, gathered, NT).reshape(count_ka, owned // count_ka, count_ja * owned)
    gram_two = pick(rows, ka, 0)
    for t in range(1, count_ka):
        gram_two = gram_two + xor_permute(pick(rows, ka ^ t, 0).astype(BF16), "ka", t).astype(F32)
    gram_two = gram_two * (1.0 / math.sqrt(slices * count_ka * rank_one))

    cut = factor_two.reshape(owned, count_ja, -1)
    two = [pick(cut, ja, 1)]
    two += [xor_permute(pick(cut, ja ^ b, 1), "ja", b) for b in range(1, count_ja)]
    two = jnp.take(jnp.stack(two), places, axis=0).reshape(count_ja * owned, -1)
    reduced = dot1(two, gathered, TN).reshape(-1, slices, rank_one).transpose(1, 0, 2)
    return (gram_one, gram_two, reduced)


def shards(tensor, factor_one, factor_two):
    slices, owned, width = tensor.shape
    count_ja = lax.axis_size("ja")
    count_ka = lax.axis_size("ka")
    step = width // count_ja
    columns = slices * factor_one.shape[1]
    tiled = count_ja == 8 and count_ka == 4 and factor_two.shape[1] == 256
    tiled = tiled and step % 128 == 0 and owned % 128 == 0
    tiled = tiled and step % (16 * count_ka) == 0 and owned % (16 * count_ka) == 0
    tiled = tiled and owned * 128 % (16 * columns) == 0 and columns % 128 == 0
    tiled = tiled and columns == 8 * owned and owned == 128
    return (tiled_shards if tiled else plain_shards)(tensor, factor_one, factor_two)


def solution(mesh):
    in_specs = (P("ka", "ja", None), P(), P("ja", None))
    out_specs = (P(("ja", "ka"), None), P(("ja", "ka"), None), P("ka", "ja", None))
    return jax.shard_map(shards, mesh=mesh, in_specs=in_specs, out_specs=out_specs, check_vma=False)
```

```python
import functools
import math

import jax
import jax.numpy as jnp
from jax import lax
from jax.experimental import pallas as pl
from jax.experimental.pallas import tpu as pltpu
from jax.sharding import PartitionSpec as P

F32 = jnp.float32
BF16 = jnp.bfloat16
NN = (((1,), (0,)), ((), ()))
NT = (((1,), (1,)), ((), ()))
TN = (((0,), (0,)), ((), ()))
VMEM = pl.BlockSpec(memory_space=pltpu.VMEM)
ANY = pl.BlockSpec(memory_space=pl.ANY)


def halves(x):
    high = x.astype(BF16)
    return high, (x - high.astype(F32)).astype(BF16)


def dot1(a, b, dims):
    return lax.dot_general(a, b, dims, preferred_element_type=F32)


def dot3(a, b, dims):
    return dot1(a[0], b[0], dims) + (dot1(a[0], b[1], dims) + dot1(a[1], b[0], dims))


def call(kernel, name, outs, in_specs, *args, scratch=(), vmem=4, flops=0):
    return pl.pallas_call(
        kernel,
        out_shape=[jax.ShapeDtypeStruct(s, d) for s, d in outs],
        in_specs=in_specs,
        out_specs=[VMEM] * len(outs),
        scratch_shapes=list(scratch),
        compiler_params=pltpu.CompilerParams(vmem_limit_bytes=vmem * 1024 * 1024),
        cost_estimate=pl.CostEstimate(flops=flops, bytes_accessed=0, transcendentals=0),
        name=name,
    )(*args)


def position():
    ja = lax.axis_index("ja")
    return lax.rem(ja, 2), lax.div(ja, 2), lax.axis_index("ka"), ja


def gram_rows(core, x_ref, groups, step, keep):
    slices, owned, width = x_ref.shape
    at = [pl.multiple_of((2 * g + core) * step, step) for g in range(groups)]
    left = [x_ref[:, :, pl.ds(a, step)].reshape(slices * owned, step) for a in at]
    left = halves(jnp.concatenate(left, axis=1).T)
    wide = min(256, width)
    for n in range(0, width, wide):
        right = halves(x_ref[:, :, n : n + wide].reshape(slices * owned, wide))
        keep(slice(n, n + wide), dot3(left, right, NN).reshape(groups, step, wide))


def away_kernel(x_ref, away_ref):
    groups, step, _ = away_ref.shape

    def keep(at, rows):
        away_ref[:, :, at] = rows.astype(BF16)

    gram_rows(1 - position()[0], x_ref, groups, step, keep)


def core_kernel(x_ref, f_ref, two_ref, _, near_ref, far_ref):
    slices, owned, _ = x_ref.shape
    rank = f_ref.shape[1]
    high = far_ref.shape[0] - owned
    other = 1 - lax.div(position()[1], 2)
    chunk = two_ref[:, pl.ds(pl.multiple_of(other * 128, 128), 128)]
    for q in range(owned // high):
        far_ref[owned:, q * 128 : (q + 1) * 128] = chunk[q * high : (q + 1) * high]
    f = halves(f_ref[...])
    for k in range(slices):
        core = dot3(halves(x_ref[k]), f, NN).astype(BF16)
        at = slice(k * rank, (k + 1) * rank)
        near_ref[:owned, at] = core
        far_ref[:owned, at] = core


def home_kernel(x_ref, came_ref, _, own_ref, keep1_ref, keep2_ref, to1_ref, to2_ref, rows_ref):
    groups, step, _ = came_ref.shape
    block = own_ref.shape[1]
    lower, upper = slice(0, groups // 2), slice(groups // 2, groups)

    def keep(at, rows):
        rows_ref[...] = rows + came_ref[:, :, at].astype(F32)

        def part(chips, t):
            return rows_ref[chips, pl.ds(pl.multiple_of((position()[2] ^ t) * block, block), block)]

        own_ref[:, :, at] = part(slice(0, groups), 0)
        keep1_ref[:, :, at] = part(upper, 1)
        keep2_ref[:, :, at] = part(lower, 2)
        for i, t in enumerate((1, 3)):
            to1_ref[i, :, :, at] = part(lower, t).astype(BF16)
        for i, t in enumerate((2, 3)):
            to2_ref[i, :, :, at] = part(upper, t).astype(BF16)

    gram_rows(position()[0], x_ref, groups, step, keep)


def middle_kernel(own_ref, keep1_ref, keep2_ref, from1_ref, from2_ref, sum_ref, to1_ref, to2_ref):
    half = from1_ref.shape[1]
    count = half * from1_ref.shape[2]
    for out, keep, came in ((to1_ref, keep1_ref, from2_ref), (to2_ref, keep2_ref, from1_ref)):
        out[:count] = (keep[...] + came[1].astype(F32)).astype(BF16).reshape(count, out.shape[1])
        out[count:] = jnp.zeros((out.shape[0] - count, out.shape[1]), BF16)
    sum_ref[:half] = own_ref[:half] + from1_ref[0].astype(F32)
    sum_ref[half:] = own_ref[half:] + from2_ref[0].astype(F32)


def slab_kernel(sum_ref, from1_ref, from2_ref, mine_ref, came_ref, *refs):
    *outs, part_ref, rows_ref = refs
    half, height = sum_ref.shape[0] // 2, sum_ref.shape[1]
    count = half * height
    part = part_ref.shape[0]
    came = [ref[:count].astype(F32).reshape(half, height, ref.shape[1]) for ref in (from1_ref, from2_ref)]
    rows_ref[:half] = sum_ref[:half] + came[1]
    rows_ref[half:] = sum_ref[half:] + came[0]
    for t, out in enumerate(outs):
        out[:height] = rows_ref[position()[1] ^ t].astype(out.dtype)
    part_ref[...] = mine_ref[:part] + came_ref[:part].astype(F32)
    high, low = halves(mine_ref[part:] + came_ref[part:].astype(F32))
    outs[1][height : height + part] = high
    outs[1][height + part :] = low


def near_kernel(u, paired, got, mine_ref, other_ref):
    owned = mine_ref.shape[0]
    left = jnp.concatenate([u[:owned], paired[:owned]], axis=0)
    for t, block in enumerate((u, got)):
        rows = dot1(left, block[:owned], NT)
        at = slice(t * owned, (t + 1) * owned)
        mine_ref[:, at] = rows[:owned]
        other_ref[:, at] = rows[owned:].astype(BF16)


def cross_kernel(u, paired, got, got_paired, far, _, mine_ref, other_ref, send_ref):
    owned = mine_ref.shape[0]
    left = [ref[:owned] for ref in (u, paired, got, got_paired)]
    rows = dot1(jnp.concatenate(left, axis=0), far[:owned], NT)
    mine_ref[...] = rows[:owned]
    other_ref[...] = rows[owned : 2 * owned].astype(BF16)
    send_ref[...] = rows[2 * owned :].astype(BF16)


def merge_kernel(mine_near, other_near, mine_far, other_far, came, _, mine_ref, other_ref):
    owned, before = mine_near.shape
    half, wide = owned // 2, mine_ref.shape[1]
    mine_ref[:, :before] = mine_near[...]
    mine_ref[:, before : before + owned] = mine_far[...]
    mine_ref[:, before + owned :] = came[:owned].astype(F32)
    for i in range(2):
        at, start = slice(i * half, (i + 1) * half), i * wide
        other_ref[:, start : start + before] = other_near[at]
        other_ref[:, start + before : start + before + owned] = other_far[at]
        other_ref[:, start + before + owned : start + wide] = came[owned + i * half : owned + (i + 1) * half]


def parts_kernel(u, far, two_ref, _, mine_ref, other_ref, sum_ref):
    owned = two_ref.shape[0]
    part = mine_ref.shape[0] // 2
    high = far.shape[0] - owned
    _, z, _, ja = position()
    own = two_ref[:, pl.ds(pl.multiple_of(lax.div(z, 2) * 128, 128), 128)]
    chunk = [far[owned:, q * 128 : (q + 1) * 128] for q in range(owned // high)]
    sum_ref[...] = dot1(own, u[:owned], TN) + dot1(jnp.concatenate(chunk, axis=0), far[:owned], TN)
    for t in range(4):
        start = pl.multiple_of(lax.rem(ja ^ t, 4) * part, part)
        out = (mine_ref, other_ref)[t % 2]
        out[t // 2 * part : (t // 2 + 1) * part] = sum_ref[pl.ds(start, part)].astype(out.dtype)


def place_kernel(mine, came, *outs):
    _, *outs, rows_ref = outs
    owned, wide = mine.shape
    half = owned // 2
    for t in range(wide // owned):
        at = pl.multiple_of((position()[3] ^ (2 * t)) * owned, owned)
        rows_ref[:, pl.ds(at, owned)] = mine[:, t * owned : (t + 1) * owned]
        at = pl.multiple_of((position()[3] ^ (2 * t + 1)) * owned, owned)
        for i in range(2):
            part = came[:, i * wide + t * owned : i * wide + (t + 1) * owned]
            rows_ref[i * half : (i + 1) * half, pl.ds(at, owned)] = part.astype(F32)
    height = owned // len(outs)
    for t, out in enumerate(outs):
        at = pl.multiple_of((position()[2] ^ t) * height, height)
        out[...] = rows_ref[pl.ds(at, height)].astype(out.dtype)


def one_kernel(scale, mine, *refs):
    *parts, one_ref, reduced_ref, done_ref = refs
    done_ref[...] = jnp.zeros_like(done_ref)
    second = parts[1]
    total = parts[0][...]
    height = total.shape[0]
    for part in parts[1:]:
        total = total + part[:height].astype(F32)
    one_ref[...] = total * scale
    slices, part, rank = reduced_ref.shape
    for k in range(slices):
        at = slice(k * rank, (k + 1) * rank)
        came = second[height : height + part, at].astype(F32) + second[height + part :, at].astype(F32)
        reduced_ref[k] = mine[:, at] + came


def two_kernel(scale, count, *refs):
    parts, out_ref = refs[:count], refs[-1]
    total = parts[0][...]
    for part in parts[1:]:
        total = total + part[...].astype(F32)
    out_ref[...] = total * scale


def xor_permute(x, axis, bits):
    return lax.ppermute(x, axis, [(i, i ^ bits) for i in range(lax.axis_size(axis))])


def pick(x, index, axis):
    return lax.dynamic_index_in_dim(x, index, axis, keepdims=False)


def tiled_shards(tensor, factor_one, factor_two):
    slices, owned, width = tensor.shape
    count_ja = lax.axis_size("ja")
    count_ka = lax.axis_size("ka")
    count_z = count_ja // 2
    rank_one = factor_one.shape[1]
    part = factor_two.shape[1] // count_ja
    step = width // count_ja
    columns = slices * rank_one
    high = owned * 128 // columns
    norm_one = 1.0 / math.sqrt(owned * count_ja * slices * count_ka)
    norm_two = 1.0 / math.sqrt(slices * count_ka * rank_one)

    (away,) = call(
        away_kernel, "away", [((count_z, step, width), BF16)], [VMEM], tensor, vmem=4
    )
    near, far = call(
        core_kernel,
        "core",
        [((owned, columns), BF16), ((owned + high, columns), BF16)],
        [VMEM, VMEM, VMEM, ANY],
        tensor,
        factor_one,
        factor_two,
        away,
        vmem=4,
    )

    far2 = xor_permute(far, "ja", 4)
    got1 = xor_permute(near, "ja", 2)
    paired = xor_permute(near, "ja", 1)
    came = xor_permute(away, "ja", 1)

    shape = (count_z, step // count_ka, width)
    half = (count_z // 2, *shape[1:])
    own, keep1, keep2, to1, to2 = call(
        home_kernel,
        "home",
        [(shape, F32), (half, F32), (half, F32), ((2, *half), BF16), ((2, *half), BF16)],
        [VMEM, VMEM, ANY],
        tensor,
        came,
        paired,
        scratch=[pltpu.VMEM((count_z, step, min(256, width)), F32)],
        vmem=6,
    )
    from1 = xor_permute(to1, "ka", 1)
    from2 = xor_permute(to2, "ka", 2)
    total, to1, to2 = call(
        middle_kernel,
        "middle",
        [(shape, F32)] + [((half[0] * half[1] + 16, width), BF16)] * 2,
        [VMEM] * 5,
        own,
        keep1,
        keep2,
        from1,
        from2,
    )
    from1 = xor_permute(to1, "ka", 1)
    from2 = xor_permute(to2, "ka", 2)
    got_paired = xor_permute(got1, "ja", 1)
    first = call(
        near_kernel,
        "two_near",
        [((owned, 2 * owned), F32), ((owned, 2 * owned), BF16)],
        [VMEM] * 3,
        near,
        paired,
        got1,
    )
    *second, send = call(
        cross_kernel,
        "two_cross",
        [((owned, owned), F32), ((owned, owned), BF16), ((2 * owned, owned), BF16)],
        [VMEM] * 5 + [ANY],
        near,
        paired,
        got1,
        got_paired,
        far2,
        total,
    )
    crossed = xor_permute(send, "ja", 2)
    mine_part, other_part = call(
        parts_kernel,
        "parts",
        [((2 * part, columns), F32), ((2 * part, columns), BF16)],
        [VMEM] * 3 + [ANY],
        near,
        far2,
        factor_two,
        send,
        scratch=[pltpu.VMEM((128, columns), F32)],
    )
    height = step // count_ka
    *sums, mine_part = call(
        slab_kernel,
        "slab",
        [
            ((height + (2 * part if t == 1 else 0), width), F32 if t == 0 else BF16)
            for t in range(count_z)
        ]
        + [((part, columns), F32)],
        [VMEM] * 5,
        total,
        from1,
        from2,
        mine_part,
        xor_permute(other_part, "ja", 1),
        scratch=[pltpu.VMEM(shape, F32)],
    )
    sums = list(sums)
    for t in reversed(range(1, count_z)):
        sums[t] = xor_permute(sums[t], "ja", 2 * t)
    mine, other = call(
        merge_kernel,
        "two_merge",
        [((owned, 4 * owned), F32), ((owned // 2, 8 * owned), BF16)],
        [VMEM] * 5 + [ANY],
        *first,
        *second,
        crossed,
        sums[0],
    )
    other = xor_permute(other, "ja", 1)
    final = (owned // count_ka, count_ja * owned)
    rows = call(
        place_kernel,
        "two_place",
        [(final, F32 if t == 0 else BF16) for t in range(count_ka)],
        [VMEM] * 2 + [ANY],
        mine,
        other,
        sums[1],
        scratch=[pltpu.VMEM((owned, count_ja * owned), F32)],
    )
    rows = list(rows)
    for t in range(1, count_ka):
        rows[t] = xor_permute(rows[t], "ka", t)
    gram_one, reduced, done = call(
        functools.partial(one_kernel, norm_one),
        "one",
        [((height, width), F32), ((slices, part, rank_one), F32), ((8, 128), F32)],
        [VMEM] * (1 + count_z),
        mine_part,
        *sums,
        flops=0,
    )
    (gram_two,) = call(
        functools.partial(two_kernel, norm_two, count_ka),
        "two",
        [(final, F32)],
        [VMEM] * count_ka + [ANY],
        *rows,
        done,
    )
    return gram_one, gram_two, reduced


def plain_shards(tensor, factor_one, factor_two):
    slices, owned, width = tensor.shape
    count_ja = lax.axis_size("ja")
    count_ka = lax.axis_size("ka")
    count_z = count_ja // 2
    rank_one = factor_one.shape[1]
    ja = lax.axis_index("ja")
    ka = lax.axis_index("ka")
    core_at, z = lax.rem(ja, 2), lax.div(ja, 2)
    step = width // count_ja
    x = halves(tensor.reshape(slices * owned, width))
    core = dot3(x, halves(factor_one), NN).astype(BF16).reshape(slices, owned, rank_one)
    u = core.transpose(1, 0, 2).reshape(owned, slices * rank_one)
    local = dot3(x, x, TN).reshape(count_z, 2, step, width)
    home = pick(local, core_at, 1)
    home = home + xor_permute(pick(local, 1 - core_at, 1).astype(BF16), "ja", 1).astype(F32)
    home = home.reshape(count_z, count_ka, step // count_ka, width)
    slab = pick(home, ka, 1)
    for t in range(1, count_ka):
        slab = slab + xor_permute(pick(home, ka ^ t, 1).astype(BF16), "ka", t).astype(F32)
    gram_one = pick(slab, z, 0)
    for t in range(1, count_z):
        gram_one = gram_one + xor_permute(pick(slab, z ^ t, 0).astype(BF16), "ja", 2 * t).astype(F32)
    gram_one = gram_one * (1.0 / math.sqrt(owned * count_ja * slices * count_ka))

    blocks = [u, xor_permute(u, "ja", 1)]
    for t in range(1, count_z):
        block = xor_permute(u, "ja", 2 * t)
        blocks += [block, xor_permute(block, "ja", 1)]
    places = jnp.arange(count_ja) ^ ja
    gathered = jnp.take(jnp.stack(blocks), places, axis=0).reshape(count_ja * owned, -1)
    rows = dot1(u, gathered, NT).reshape(count_ka, owned // count_ka, count_ja * owned)
    gram_two = pick(rows, ka, 0)
    for t in range(1, count_ka):
        gram_two = gram_two + xor_permute(pick(rows, ka ^ t, 0).astype(BF16), "ka", t).astype(F32)
    gram_two = gram_two * (1.0 / math.sqrt(slices * count_ka * rank_one))

    cut = factor_two.reshape(owned, count_ja, -1)
    two = [pick(cut, ja, 1)]
    two += [xor_permute(pick(cut, ja ^ b, 1), "ja", b) for b in range(1, count_ja)]
    two = jnp.take(jnp.stack(two), places, axis=0).reshape(count_ja * owned, -1)
    reduced = dot1(two, gathered, TN).reshape(-1, slices, rank_one).transpose(1, 0, 2)
    return (gram_one, gram_two, reduced)


def shards(tensor, factor_one, factor_two):
    slices, owned, width = tensor.shape
    count_ja = lax.axis_size("ja")
    count_ka = lax.axis_size("ka")
    step = width // count_ja
    columns = slices * factor_one.shape[1]
    tiled = count_ja == 8 and count_ka == 4 and factor_two.shape[1] == 256
    tiled = tiled and step % 128 == 0 and owned % 128 == 0
    tiled = tiled and step % (16 * count_ka) == 0 and owned % (16 * count_ka) == 0
    tiled = tiled and owned * 128 % (16 * columns) == 0 and columns % 128 == 0
    tiled = tiled and columns == 8 * owned and owned == 128
    return (tiled_shards if tiled else plain_shards)(tensor, factor_one, factor_two)


def solution(mesh):
    in_specs = (P("ka", "ja", None), P(), P("ja", None))
    out_specs = (P(("ja", "ka"), None), P(("ja", "ka"), None), P("ka", "ja", None))
    return jax.shard_map(shards, mesh=mesh, in_specs=in_specs, out_specs=out_specs, check_vma=False)
```

```python
import functools
import math

import jax
import jax.numpy as jnp
from jax import lax
from jax.experimental import pallas as pl
from jax.experimental.pallas import tpu as pltpu
from jax.sharding import PartitionSpec as P

F32 = jnp.float32
BF16 = jnp.bfloat16
NN = (((1,), (0,)), ((), ()))
NT = (((1,), (1,)), ((), ()))
TN = (((0,), (0,)), ((), ()))
VMEM = pl.BlockSpec(memory_space=pltpu.VMEM)
ANY = pl.BlockSpec(memory_space=pl.ANY)


def halves(x):
    high = x.astype(BF16)
    return high, (x - high.astype(F32)).astype(BF16)


def dot1(a, b, dims):
    return lax.dot_general(a, b, dims, preferred_element_type=F32)


def dot3(a, b, dims):
    return dot1(a[0], b[0], dims) + (dot1(a[0], b[1], dims) + dot1(a[1], b[0], dims))


def call(kernel, name, outs, in_specs, *args, scratch=(), vmem=4, flops=0):
    return pl.pallas_call(
        kernel,
        out_shape=[jax.ShapeDtypeStruct(s, d) for s, d in outs],
        in_specs=in_specs,
        out_specs=[VMEM] * len(outs),
        scratch_shapes=list(scratch),
        compiler_params=pltpu.CompilerParams(vmem_limit_bytes=vmem * 1024 * 1024),
        cost_estimate=pl.CostEstimate(flops=flops, bytes_accessed=0, transcendentals=0),
        name=name,
    )(*args)


def position():
    ja = lax.axis_index("ja")
    return lax.rem(ja, 2), lax.div(ja, 2), lax.axis_index("ka"), ja


def gram_rows(core, x_ref, groups, step, keep):
    slices, owned, width = x_ref.shape
    at = [pl.multiple_of((2 * g + core) * step, step) for g in range(groups)]
    left = [x_ref[:, :, pl.ds(a, step)].reshape(slices * owned, step) for a in at]
    left = halves(jnp.concatenate(left, axis=1).T)
    wide = min(256, width)
    for n in range(0, width, wide):
        right = halves(x_ref[:, :, n : n + wide].reshape(slices * owned, wide))
        keep(slice(n, n + wide), dot3(left, right, NN).reshape(groups, step, wide))


def away_kernel(x_ref, away_ref):
    groups, step, _ = away_ref.shape

    def keep(at, rows):
        away_ref[:, :, at] = rows.astype(BF16)

    gram_rows(1 - position()[0], x_ref, groups, step, keep)


def core_kernel(x_ref, f_ref, two_ref, _, near_ref, far_ref):
    slices, owned, _ = x_ref.shape
    rank = f_ref.shape[1]
    high = far_ref.shape[0] - owned
    other = 1 - lax.div(position()[1], 2)
    chunk = two_ref[:, pl.ds(pl.multiple_of(other * 128, 128), 128)]
    for q in range(owned // high):
        far_ref[owned:, q * 128 : (q + 1) * 128] = chunk[q * high : (q + 1) * high]
    f = halves(f_ref[...])
    for k in range(slices):
        core = dot3(halves(x_ref[k]), f, NN).astype(BF16)
        at = slice(k * rank, (k + 1) * rank)
        near_ref[:owned, at] = core
        far_ref[:owned, at] = core


def home_kernel(x_ref, came_ref, _, own_ref, keep1_ref, keep2_ref, to1_ref, to2_ref, rows_ref):
    groups, step, _ = came_ref.shape
    block = own_ref.shape[1]
    lower, upper = slice(0, groups // 2), slice(groups // 2, groups)

    def keep(at, rows):
        rows_ref[...] = rows + came_ref[:, :, at].astype(F32)

        def part(chips, t):
            return rows_ref[chips, pl.ds(pl.multiple_of((position()[2] ^ t) * block, block), block)]

        own_ref[:, :, at] = part(slice(0, groups), 0)
        keep1_ref[:, :, at] = part(upper, 1)
        keep2_ref[:, :, at] = part(lower, 2)
        for i, t in enumerate((1, 3)):
            to1_ref[i, :, :, at] = part(lower, t).astype(BF16)
        for i, t in enumerate((2, 3)):
            to2_ref[i, :, :, at] = part(upper, t).astype(BF16)

    gram_rows(position()[0], x_ref, groups, step, keep)


def middle_kernel(own_ref, keep1_ref, keep2_ref, from1_ref, from2_ref, sum_ref, to1_ref, to2_ref):
    half = from1_ref.shape[1]
    count = half * from1_ref.shape[2]
    for out, keep, came in ((to1_ref, keep1_ref, from2_ref), (to2_ref, keep2_ref, from1_ref)):
        out[:count] = (keep[...] + came[1].astype(F32)).astype(BF16).reshape(count, out.shape[1])
        out[count:] = jnp.zeros((out.shape[0] - count, out.shape[1]), BF16)
    sum_ref[:half] = own_ref[:half] + from1_ref[0].astype(F32)
    sum_ref[half:] = own_ref[half:] + from2_ref[0].astype(F32)


def slab_kernel(sum_ref, from1_ref, from2_ref, mine_ref, came_ref, *refs):
    *outs, part_ref, rows_ref = refs
    half, height = sum_ref.shape[0] // 2, sum_ref.shape[1]
    count = half * height
    part = part_ref.shape[0]
    came = [ref[:count].astype(F32).reshape(half, height, ref.shape[1]) for ref in (from1_ref, from2_ref)]
    rows_ref[:half] = sum_ref[:half] + came[1]
    rows_ref[half:] = sum_ref[half:] + came[0]
    for t, out in enumerate(outs):
        out[:height] = rows_ref[position()[1] ^ t].astype(out.dtype)
    part_ref[...] = mine_ref[:part] + came_ref[:part].astype(F32)
    outs[1][height : height + part] = (mine_ref[part:] + came_ref[part:].astype(F32)).astype(BF16)
    outs[1][height + part :] = jnp.zeros((part // 2, outs[1].shape[1]), BF16)


def near_kernel(u, paired, got, mine_ref, other_ref):
    owned = mine_ref.shape[0]
    left = jnp.concatenate([u[:owned], paired[:owned]], axis=0)
    for t, block in enumerate((u, got)):
        rows = dot1(left, block[:owned], NT)
        at = slice(t * owned, (t + 1) * owned)
        mine_ref[:, at] = rows[:owned]
        other_ref[:, at] = rows[owned:].astype(BF16)


def cross_kernel(u, paired, got, got_paired, far, _, mine_ref, other_ref, send_ref):
    owned = mine_ref.shape[0]
    left = [ref[:owned] for ref in (u, paired, got, got_paired)]
    rows = dot1(jnp.concatenate(left, axis=0), far[:owned], NT)
    mine_ref[...] = rows[:owned]
    other_ref[...] = rows[owned : 2 * owned].astype(BF16)
    send_ref[...] = rows[2 * owned :].astype(BF16)


def merge_kernel(mine_near, other_near, mine_far, other_far, came, _, mine_ref, other_ref):
    owned, before = mine_near.shape
    half, wide = owned // 2, mine_ref.shape[1]
    mine_ref[:, :before] = mine_near[...]
    mine_ref[:, before : before + owned] = mine_far[...]
    mine_ref[:, before + owned :] = came[:owned].astype(F32)
    for i in range(2):
        at, start = slice(i * half, (i + 1) * half), i * wide
        other_ref[:, start : start + before] = other_near[at]
        other_ref[:, start + before : start + before + owned] = other_far[at]
        other_ref[:, start + before + owned : start + wide] = came[owned + i * half : owned + (i + 1) * half]


def parts_kernel(u, far, two_ref, _, mine_ref, other_ref, sum_ref):
    owned = two_ref.shape[0]
    part = mine_ref.shape[0] // 2
    high = far.shape[0] - owned
    _, z, _, ja = position()
    own = two_ref[:, pl.ds(pl.multiple_of(lax.div(z, 2) * 128, 128), 128)]
    chunk = [far[owned:, q * 128 : (q + 1) * 128] for q in range(owned // high)]
    sum_ref[...] = dot1(own, u[:owned], TN) + dot1(jnp.concatenate(chunk, axis=0), far[:owned], TN)
    for t in range(4):
        start = pl.multiple_of(lax.rem(ja ^ t, 4) * part, part)
        out = (mine_ref, other_ref)[t % 2]
        out[t // 2 * part : (t // 2 + 1) * part] = sum_ref[pl.ds(start, part)].astype(out.dtype)


def place_kernel(mine, came, *outs):
    _, *outs, rows_ref = outs
    owned, wide = mine.shape
    half = owned // 2
    for t in range(wide // owned):
        at = pl.multiple_of((position()[3] ^ (2 * t)) * owned, owned)
        rows_ref[:, pl.ds(at, owned)] = mine[:, t * owned : (t + 1) * owned]
        at = pl.multiple_of((position()[3] ^ (2 * t + 1)) * owned, owned)
        for i in range(2):
            part = came[:, i * wide + t * owned : i * wide + (t + 1) * owned]
            rows_ref[i * half : (i + 1) * half, pl.ds(at, owned)] = part.astype(F32)
    height = owned // len(outs)
    for t, out in enumerate(outs):
        at = pl.multiple_of((position()[2] ^ t) * height, height)
        out[...] = rows_ref[pl.ds(at, height)].astype(out.dtype)


def one_kernel(scale, mine, *refs):
    *parts, one_ref, reduced_ref, done_ref = refs
    done_ref[...] = jnp.zeros_like(done_ref)
    second = parts[1]
    total = parts[0][...]
    height = total.shape[0]
    for part in parts[1:]:
        total = total + part[:height].astype(F32)
    one_ref[...] = total * scale
    slices, part, rank = reduced_ref.shape
    for k in range(slices):
        at = slice(k * rank, (k + 1) * rank)
        came = second[height : height + part, at].astype(F32)
        reduced_ref[k] = mine[:, at] + came


def two_kernel(scale, count, *refs):
    parts, out_ref = refs[:count], refs[-1]
    total = parts[0][...]
    for part in parts[1:]:
        total = total + part[...].astype(F32)
    out_ref[...] = total * scale


def xor_permute(x, axis, bits):
    return lax.ppermute(x, axis, [(i, i ^ bits) for i in range(lax.axis_size(axis))])


def pick(x, index, axis):
    return lax.dynamic_index_in_dim(x, index, axis, keepdims=False)


def tiled_shards(tensor, factor_one, factor_two):
    slices, owned, width = tensor.shape
    count_ja = lax.axis_size("ja")
    count_ka = lax.axis_size("ka")
    count_z = count_ja // 2
    rank_one = factor_one.shape[1]
    part = factor_two.shape[1] // count_ja
    step = width // count_ja
    columns = slices * rank_one
    high = owned * 128 // columns
    norm_one = 1.0 / math.sqrt(owned * count_ja * slices * count_ka)
    norm_two = 1.0 / math.sqrt(slices * count_ka * rank_one)

    (away,) = call(
        away_kernel, "away", [((count_z, step, width), BF16)], [VMEM], tensor, vmem=4
    )
    near, far = call(
        core_kernel,
        "core",
        [((owned, columns), BF16), ((owned + high, columns), BF16)],
        [VMEM, VMEM, VMEM, ANY],
        tensor,
        factor_one,
        factor_two,
        away,
        vmem=4,
    )

    far2 = xor_permute(far, "ja", 4)
    got1 = xor_permute(near, "ja", 2)
    paired = xor_permute(near, "ja", 1)
    came = xor_permute(away, "ja", 1)

    shape = (count_z, step // count_ka, width)
    half = (count_z // 2, *shape[1:])
    own, keep1, keep2, to1, to2 = call(
        home_kernel,
        "home",
        [(shape, F32), (half, F32), (half, F32), ((2, *half), BF16), ((2, *half), BF16)],
        [VMEM, VMEM, ANY],
        tensor,
        came,
        paired,
        scratch=[pltpu.VMEM((count_z, step, min(256, width)), F32)],
        vmem=6,
    )
    from1 = xor_permute(to1, "ka", 1)
    from2 = xor_permute(to2, "ka", 2)
    total, to1, to2 = call(
        middle_kernel,
        "middle",
        [(shape, F32)] + [((half[0] * half[1] + 16, width), BF16)] * 2,
        [VMEM] * 5,
        own,
        keep1,
        keep2,
        from1,
        from2,
    )
    from1 = xor_permute(to1, "ka", 1)
    from2 = xor_permute(to2, "ka", 2)
    got_paired = xor_permute(got1, "ja", 1)
    first = call(
        near_kernel,
        "two_near",
        [((owned, 2 * owned), F32), ((owned, 2 * owned), BF16)],
        [VMEM] * 3,
        near,
        paired,
        got1,
    )
    *second, send = call(
        cross_kernel,
        "two_cross",
        [((owned, owned), F32), ((owned, owned), BF16), ((2 * owned, owned), BF16)],
        [VMEM] * 5 + [ANY],
        near,
        paired,
        got1,
        got_paired,
        far2,
        total,
    )
    crossed = xor_permute(send, "ja", 2)
    mine_part, other_part = call(
        parts_kernel,
        "parts",
        [((2 * part, columns), F32), ((2 * part, columns), BF16)],
        [VMEM] * 3 + [ANY],
        near,
        far2,
        factor_two,
        send,
        scratch=[pltpu.VMEM((128, columns), F32)],
    )
    height = step // count_ka
    *sums, mine_part = call(
        slab_kernel,
        "slab",
        [
            ((height + (part + part // 2 if t == 1 else 0), width), F32 if t == 0 else BF16)
            for t in range(count_z)
        ]
        + [((part, columns), F32)],
        [VMEM] * 5,
        total,
        from1,
        from2,
        mine_part,
        xor_permute(other_part, "ja", 1),
        scratch=[pltpu.VMEM(shape, F32)],
    )
    sums = list(sums)
    for t in reversed(range(1, count_z)):
        sums[t] = xor_permute(sums[t], "ja", 2 * t)
    mine, other = call(
        merge_kernel,
        "two_merge",
        [((owned, 4 * owned), F32), ((owned // 2, 8 * owned), BF16)],
        [VMEM] * 5 + [ANY],
        *first,
        *second,
        crossed,
        sums[0],
    )
    other = xor_permute(other, "ja", 1)
    final = (owned // count_ka, count_ja * owned)
    rows = call(
        place_kernel,
        "two_place",
        [(final, F32 if t == 0 else BF16) for t in range(count_ka)],
        [VMEM] * 2 + [ANY],
        mine,
        other,
        sums[1],
        scratch=[pltpu.VMEM((owned, count_ja * owned), F32)],
    )
    rows = list(rows)
    for t in range(1, count_ka):
        rows[t] = xor_permute(rows[t], "ka", t)
    gram_one, reduced, done = call(
        functools.partial(one_kernel, norm_one),
        "one",
        [((height, width), F32), ((slices, part, rank_one), F32), ((8, 128), F32)],
        [VMEM] * (1 + count_z),
        mine_part,
        *sums,
        flops=0,
    )
    (gram_two,) = call(
        functools.partial(two_kernel, norm_two, count_ka),
        "two",
        [(final, F32)],
        [VMEM] * count_ka + [ANY],
        *rows,
        done,
    )
    return gram_one, gram_two, reduced


def plain_shards(tensor, factor_one, factor_two):
    slices, owned, width = tensor.shape
    count_ja = lax.axis_size("ja")
    count_ka = lax.axis_size("ka")
    count_z = count_ja // 2
    rank_one = factor_one.shape[1]
    ja = lax.axis_index("ja")
    ka = lax.axis_index("ka")
    core_at, z = lax.rem(ja, 2), lax.div(ja, 2)
    step = width // count_ja
    x = halves(tensor.reshape(slices * owned, width))
    core = dot3(x, halves(factor_one), NN).astype(BF16).reshape(slices, owned, rank_one)
    u = core.transpose(1, 0, 2).reshape(owned, slices * rank_one)
    local = dot3(x, x, TN).reshape(count_z, 2, step, width)
    home = pick(local, core_at, 1)
    home = home + xor_permute(pick(local, 1 - core_at, 1).astype(BF16), "ja", 1).astype(F32)
    home = home.reshape(count_z, count_ka, step // count_ka, width)
    slab = pick(home, ka, 1)
    for t in range(1, count_ka):
        slab = slab + xor_permute(pick(home, ka ^ t, 1).astype(BF16), "ka", t).astype(F32)
    gram_one = pick(slab, z, 0)
    for t in range(1, count_z):
        gram_one = gram_one + xor_permute(pick(slab, z ^ t, 0).astype(BF16), "ja", 2 * t).astype(F32)
    gram_one = gram_one * (1.0 / math.sqrt(owned * count_ja * slices * count_ka))

    blocks = [u, xor_permute(u, "ja", 1)]
    for t in range(1, count_z):
        block = xor_permute(u, "ja", 2 * t)
        blocks += [block, xor_permute(block, "ja", 1)]
    places = jnp.arange(count_ja) ^ ja
    gathered = jnp.take(jnp.stack(blocks), places, axis=0).reshape(count_ja * owned, -1)
    rows = dot1(u, gathered, NT).reshape(count_ka, owned // count_ka, count_ja * owned)
    gram_two = pick(rows, ka, 0)
    for t in range(1, count_ka):
        gram_two = gram_two + xor_permute(pick(rows, ka ^ t, 0).astype(BF16), "ka", t).astype(F32)
    gram_two = gram_two * (1.0 / math.sqrt(slices * count_ka * rank_one))

    cut = factor_two.reshape(owned, count_ja, -1)
    two = [pick(cut, ja, 1)]
    two += [xor_permute(pick(cut, ja ^ b, 1), "ja", b) for b in range(1, count_ja)]
    two = jnp.take(jnp.stack(two), places, axis=0).reshape(count_ja * owned, -1)
    reduced = dot1(two, gathered, TN).reshape(-1, slices, rank_one).transpose(1, 0, 2)
    return (gram_one, gram_two, reduced)


def shards(tensor, factor_one, factor_two):
    slices, owned, width = tensor.shape
    count_ja = lax.axis_size("ja")
    count_ka = lax.axis_size("ka")
    step = width // count_ja
    columns = slices * factor_one.shape[1]
    tiled = count_ja == 8 and count_ka == 4 and factor_two.shape[1] == 256
    tiled = tiled and step % 128 == 0 and owned % 128 == 0
    tiled = tiled and step % (16 * count_ka) == 0 and owned % (16 * count_ka) == 0
    tiled = tiled and owned * 128 % (16 * columns) == 0 and columns % 128 == 0
    tiled = tiled and columns == 8 * owned and owned == 128
    return (tiled_shards if tiled else plain_shards)(tensor, factor_one, factor_two)


def solution(mesh):
    in_specs = (P("ka", "ja", None), P(), P("ja", None))
    out_specs = (P(("ja", "ka"), None), P(("ja", "ka"), None), P("ka", "ja", None))
    return jax.shard_map(shards, mesh=mesh, in_specs=in_specs, out_specs=out_specs, check_vma=False)
```

```python
import functools
import math

import jax
import jax.numpy as jnp
from jax import lax
from jax.experimental import pallas as pl
from jax.experimental.pallas import tpu as pltpu
from jax.sharding import PartitionSpec as P

F32 = jnp.float32
BF16 = jnp.bfloat16
NN = (((1,), (0,)), ((), ()))
NT = (((1,), (1,)), ((), ()))
TN = (((0,), (0,)), ((), ()))
VMEM = pl.BlockSpec(memory_space=pltpu.VMEM)
ANY = pl.BlockSpec(memory_space=pl.ANY)


def halves(x):
    high = x.astype(BF16)
    return high, (x - high.astype(F32)).astype(BF16)


def dot1(a, b, dims):
    return lax.dot_general(a, b, dims, preferred_element_type=F32)


def dot3(a, b, dims):
    return dot1(a[0], b[0], dims) + (dot1(a[0], b[1], dims) + dot1(a[1], b[0], dims))


def call(kernel, name, outs, in_specs, *args, scratch=(), vmem=4, flops=0):
    return pl.pallas_call(
        kernel,
        out_shape=[jax.ShapeDtypeStruct(s, d) for s, d in outs],
        in_specs=in_specs,
        out_specs=[VMEM] * len(outs),
        scratch_shapes=list(scratch),
        compiler_params=pltpu.CompilerParams(vmem_limit_bytes=vmem * 1024 * 1024),
        cost_estimate=pl.CostEstimate(flops=flops, bytes_accessed=0, transcendentals=0),
        name=name,
    )(*args)


def position():
    ja = lax.axis_index("ja")
    return lax.rem(ja, 2), lax.div(ja, 2), lax.axis_index("ka"), ja


def gram_rows(core, x_ref, groups, step, keep):
    slices, owned, width = x_ref.shape
    at = [pl.multiple_of((2 * g + core) * step, step) for g in range(groups)]
    left = [x_ref[:, :, pl.ds(a, step)].reshape(slices * owned, step) for a in at]
    left = halves(jnp.concatenate(left, axis=1).T)
    wide = min(256, width)
    for n in range(0, width, wide):
        right = halves(x_ref[:, :, n : n + wide].reshape(slices * owned, wide))
        keep(slice(n, n + wide), dot3(left, right, NN).reshape(groups, step, wide))


def away_kernel(x_ref, away_ref):
    groups, step, _ = away_ref.shape

    def keep(at, rows):
        away_ref[:, :, at] = rows.astype(BF16)

    gram_rows(1 - position()[0], x_ref, groups, step, keep)


def core_kernel(x_ref, f_ref, two_ref, _, near_ref, far_ref):
    slices, owned, _ = x_ref.shape
    rank = f_ref.shape[1]
    high = far_ref.shape[0] - owned
    other = 1 - lax.div(position()[1], 2)
    chunk = two_ref[:, pl.ds(pl.multiple_of(other * 128, 128), 128)]
    for q in range(owned // high):
        far_ref[owned:, q * 128 : (q + 1) * 128] = chunk[q * high : (q + 1) * high]
    f = halves(f_ref[...])
    for k in range(slices):
        core = dot3(halves(x_ref[k]), f, NN).astype(BF16)
        at = slice(k * rank, (k + 1) * rank)
        near_ref[:owned, at] = core
        far_ref[:owned, at] = core


def home_kernel(x_ref, came_ref, _, own_ref, keep1_ref, keep2_ref, to1_ref, to2_ref, rows_ref):
    groups, step, _ = came_ref.shape
    block = own_ref.shape[1]
    lower, upper = slice(0, groups // 2), slice(groups // 2, groups)

    def keep(at, rows):
        rows_ref[...] = rows + came_ref[:, :, at].astype(F32)

        def part(chips, t):
            return rows_ref[chips, pl.ds(pl.multiple_of((position()[2] ^ t) * block, block), block)]

        own_ref[:, :, at] = part(slice(0, groups), 0)
        keep1_ref[:, :, at] = part(upper, 1)
        keep2_ref[:, :, at] = part(lower, 2)
        for i, t in enumerate((1, 3)):
            to1_ref[i, :, :, at] = part(lower, t).astype(BF16)
        for i, t in enumerate((2, 3)):
            to2_ref[i, :, :, at] = part(upper, t).astype(BF16)

    gram_rows(position()[0], x_ref, groups, step, keep)


def middle_kernel(own_ref, keep1_ref, keep2_ref, from1_ref, from2_ref, sum_ref, to1_ref, to2_ref):
    half = from1_ref.shape[1]
    count = half * from1_ref.shape[2]
    for out, keep, came in ((to1_ref, keep1_ref, from2_ref), (to2_ref, keep2_ref, from1_ref)):
        out[:count] = (keep[...] + came[1].astype(F32)).astype(BF16).reshape(count, out.shape[1])
        out[count:] = jnp.zeros((out.shape[0] - count, out.shape[1]), BF16)
    sum_ref[:half] = own_ref[:half] + from1_ref[0].astype(F32)
    sum_ref[half:] = own_ref[half:] + from2_ref[0].astype(F32)


def slab_kernel(sum_ref, from1_ref, from2_ref, mine_ref, came_ref, *refs):
    *outs, part_ref, rows_ref = refs
    half, height = sum_ref.shape[0] // 2, sum_ref.shape[1]
    count = half * height
    part = part_ref.shape[0]
    came = [ref[:count].astype(F32).reshape(half, height, ref.shape[1]) for ref in (from1_ref, from2_ref)]
    rows_ref[:half] = sum_ref[:half] + came[1]
    rows_ref[half:] = sum_ref[half:] + came[0]
    for t, out in enumerate(outs):
        out[:height] = rows_ref[position()[1] ^ t].astype(out.dtype)
    part_ref[...] = mine_ref[:part] + came_ref[:part].astype(F32)
    outs[1][height : height + part] = (mine_ref[part:] + came_ref[part:].astype(F32)).astype(BF16)
    outs[1][height + part :] = jnp.zeros((part // 2, outs[1].shape[1]), BF16)


def near_kernel(u, paired, got, mine_ref, other_ref):
    owned = mine_ref.shape[0]
    left = jnp.concatenate([u[:owned], paired[:owned]], axis=0)
    for t, block in enumerate((u, got)):
        rows = dot1(left, block[:owned], NT)
        at = slice(t * owned, (t + 1) * owned)
        mine_ref[:, at] = rows[:owned]
        other_ref[:, at] = rows[owned:].astype(BF16)


def cross_kernel(u, paired, got, got_paired, far, _, mine_ref, other_ref, send_ref):
    owned = mine_ref.shape[0]
    left = [ref[:owned] for ref in (u, paired, got, got_paired)]
    rows = dot1(jnp.concatenate(left, axis=0), far[:owned], NT)
    mine_ref[...] = rows[:owned]
    other_ref[...] = rows[owned : 2 * owned].astype(BF16)
    send_ref[...] = rows[2 * owned :].astype(BF16)


def merge_kernel(mine_near, other_near, mine_far, other_far, came, _, mine_ref, other_ref):
    owned, before = mine_near.shape
    half, wide = owned // 2, mine_ref.shape[1]
    mine_ref[:, :before] = mine_near[...]
    mine_ref[:, before : before + owned] = mine_far[...]
    mine_ref[:, before + owned :] = came[:owned].astype(F32)
    for i in range(2):
        at, start = slice(i * half, (i + 1) * half), i * wide
        other_ref[:, start : start + before] = other_near[at]
        other_ref[:, start + before : start + before + owned] = other_far[at]
        other_ref[:, start + before + owned : start + wide] = came[owned + i * half : owned + (i + 1) * half]


def parts_kernel(u, far, two_ref, _, mine_ref, other_ref, sum_ref):
    owned = two_ref.shape[0]
    part = mine_ref.shape[0] // 2
    high = far.shape[0] - owned
    _, z, _, ja = position()
    own = two_ref[:, pl.ds(pl.multiple_of(lax.div(z, 2) * 128, 128), 128)]
    chunk = [far[owned:, q * 128 : (q + 1) * 128] for q in range(owned // high)]
    sum_ref[...] = dot1(own, u[:owned], TN) + dot1(jnp.concatenate(chunk, axis=0), far[:owned], TN)
    for t in range(4):
        start = pl.multiple_of(lax.rem(ja ^ t, 4) * part, part)
        out = (mine_ref, other_ref)[t % 2]
        out[t // 2 * part : (t // 2 + 1) * part] = sum_ref[pl.ds(start, part)].astype(out.dtype)


def place_kernel(mine, came, *outs):
    _, *outs, rows_ref = outs
    owned, wide = mine.shape
    half = owned // 2
    for t in range(wide // owned):
        at = pl.multiple_of((position()[3] ^ (2 * t)) * owned, owned)
        rows_ref[:, pl.ds(at, owned)] = mine[:, t * owned : (t + 1) * owned]
        at = pl.multiple_of((position()[3] ^ (2 * t + 1)) * owned, owned)
        for i in range(2):
            part = came[:, i * wide + t * owned : i * wide + (t + 1) * owned]
            rows_ref[i * half : (i + 1) * half, pl.ds(at, owned)] = part.astype(F32)
    height = owned // len(outs)
    for t, out in enumerate(outs):
        at = pl.multiple_of((position()[2] ^ t) * height, height)
        out[...] = rows_ref[pl.ds(at, height)].astype(out.dtype)


def one_kernel(scale, mine, *refs):
    *parts, one_ref, reduced_ref, done_ref = refs
    done_ref[...] = jnp.zeros_like(done_ref)
    second = parts[1]
    total = parts[0][...]
    height = total.shape[0]
    for part in parts[1:]:
        total = total + part[:height].astype(F32)
    one_ref[...] = total * scale
    slices, part, rank = reduced_ref.shape
    for k in range(slices):
        at = slice(k * rank, (k + 1) * rank)
        came = second[height : height + part, at].astype(F32)
        reduced_ref[k] = mine[:, at] + came


def two_kernel(scale, count, *refs):
    parts, out_ref = refs[:count], refs[-1]
    total = parts[0][...]
    for part in parts[1:]:
        total = total + part[...].astype(F32)
    out_ref[...] = total * scale


def xor_permute(x, axis, bits):
    return lax.ppermute(x, axis, [(i, i ^ bits) for i in range(lax.axis_size(axis))])


def pick(x, index, axis):
    return lax.dynamic_index_in_dim(x, index, axis, keepdims=False)


def tiled_shards(tensor, factor_one, factor_two):
    slices, owned, width = tensor.shape
    count_ja = lax.axis_size("ja")
    count_ka = lax.axis_size("ka")
    count_z = count_ja // 2
    rank_one = factor_one.shape[1]
    part = factor_two.shape[1] // count_ja
    step = width // count_ja
    columns = slices * rank_one
    high = owned * 128 // columns
    norm_one = 1.0 / math.sqrt(owned * count_ja * slices * count_ka)
    norm_two = 1.0 / math.sqrt(slices * count_ka * rank_one)

    (away,) = call(
        away_kernel, "away", [((count_z, step, width), BF16)], [VMEM], tensor, vmem=4
    )
    near, far = call(
        core_kernel,
        "core",
        [((owned, columns), BF16), ((owned + high, columns), BF16)],
        [VMEM, VMEM, VMEM, ANY],
        tensor,
        factor_one,
        factor_two,
        away,
        vmem=4,
    )

    far2 = xor_permute(far, "ja", 4)
    got1 = xor_permute(near, "ja", 2)
    paired = xor_permute(near, "ja", 1)
    came = xor_permute(away, "ja", 1)

    shape = (count_z, step // count_ka, width)
    half = (count_z // 2, *shape[1:])
    own, keep1, keep2, to1, to2 = call(
        home_kernel,
        "home",
        [(shape, F32), (half, F32), (half, F32), ((2, *half), BF16), ((2, *half), BF16)],
        [VMEM, VMEM, ANY],
        tensor,
        came,
        paired,
        scratch=[pltpu.VMEM((count_z, step, min(256, width)), F32)],
        vmem=6,
    )
    from1 = xor_permute(to1, "ka", 1)
    from2 = xor_permute(to2, "ka", 2)
    total, to1, to2 = call(
        middle_kernel,
        "middle",
        [(shape, F32)] + [((half[0] * half[1] + 16, width), BF16)] * 2,
        [VMEM] * 5,
        own,
        keep1,
        keep2,
        from1,
        from2,
    )
    from1 = xor_permute(to1, "ka", 1)
    from2 = xor_permute(to2, "ka", 2)
    got_paired = xor_permute(got1, "ja", 1)
    first = call(
        near_kernel,
        "two_near",
        [((owned, 2 * owned), F32), ((owned, 2 * owned), BF16)],
        [VMEM] * 3,
        near,
        paired,
        got1,
    )
    *second, send = call(
        cross_kernel,
        "two_cross",
        [((owned, owned), F32), ((owned, owned), BF16), ((2 * owned, owned), BF16)],
        [VMEM] * 5 + [ANY],
        near,
        paired,
        got1,
        got_paired,
        far2,
        total,
    )
    crossed = xor_permute(send, "ja", 2)
    mine_part, other_part = call(
        parts_kernel,
        "parts",
        [((2 * part, columns), F32), ((2 * part, columns), BF16)],
        [VMEM] * 3 + [ANY],
        near,
        far2,
        factor_two,
        send,
        scratch=[pltpu.VMEM((128, columns), F32)],
    )
    height = step // count_ka
    *sums, mine_part = call(
        slab_kernel,
        "slab",
        [
            ((height + (part + part // 2 if t == 1 else 0), width), F32 if t == 0 else BF16)
            for t in range(count_z)
        ]
        + [((part, columns), F32)],
        [VMEM] * 5,
        total,
        from1,
        from2,
        mine_part,
        xor_permute(other_part, "ja", 1),
        scratch=[pltpu.VMEM(shape, F32)],
    )
    sums = list(sums)
    for t in reversed(range(1, count_z)):
        sums[t] = xor_permute(sums[t], "ja", 2 * t)
    mine, other = call(
        merge_kernel,
        "two_merge",
        [((owned, 4 * owned), F32), ((owned // 2, 8 * owned), BF16)],
        [VMEM] * 5 + [ANY],
        *first,
        *second,
        crossed,
        sums[0],
    )
    other = xor_permute(other, "ja", 1)
    final = (owned // count_ka, count_ja * owned)
    rows = call(
        place_kernel,
        "two_place",
        [(final, F32 if t == 0 else BF16) for t in range(count_ka)],
        [VMEM] * 2 + [ANY],
        mine,
        other,
        sums[1],
        scratch=[pltpu.VMEM((owned, count_ja * owned), F32)],
    )
    rows = list(rows)
    for t in reversed(range(1, count_ka)):
        rows[t] = xor_permute(rows[t], "ka", t)
    gram_one, reduced, done = call(
        functools.partial(one_kernel, norm_one),
        "one",
        [((height, width), F32), ((slices, part, rank_one), F32), ((8, 128), F32)],
        [VMEM] * (1 + count_z),
        mine_part,
        *sums,
        flops=0,
    )
    (gram_two,) = call(
        functools.partial(two_kernel, norm_two, count_ka),
        "two",
        [(final, F32)],
        [VMEM] * count_ka + [ANY],
        *rows,
        done,
    )
    return gram_one, gram_two, reduced


def plain_shards(tensor, factor_one, factor_two):
    slices, owned, width = tensor.shape
    count_ja = lax.axis_size("ja")
    count_ka = lax.axis_size("ka")
    count_z = count_ja // 2
    rank_one = factor_one.shape[1]
    ja = lax.axis_index("ja")
    ka = lax.axis_index("ka")
    core_at, z = lax.rem(ja, 2), lax.div(ja, 2)
    step = width // count_ja
    x = halves(tensor.reshape(slices * owned, width))
    core = dot3(x, halves(factor_one), NN).astype(BF16).reshape(slices, owned, rank_one)
    u = core.transpose(1, 0, 2).reshape(owned, slices * rank_one)
    local = dot3(x, x, TN).reshape(count_z, 2, step, width)
    home = pick(local, core_at, 1)
    home = home + xor_permute(pick(local, 1 - core_at, 1).astype(BF16), "ja", 1).astype(F32)
    home = home.reshape(count_z, count_ka, step // count_ka, width)
    slab = pick(home, ka, 1)
    for t in range(1, count_ka):
        slab = slab + xor_permute(pick(home, ka ^ t, 1).astype(BF16), "ka", t).astype(F32)
    gram_one = pick(slab, z, 0)
    for t in range(1, count_z):
        gram_one = gram_one + xor_permute(pick(slab, z ^ t, 0).astype(BF16), "ja", 2 * t).astype(F32)
    gram_one = gram_one * (1.0 / math.sqrt(owned * count_ja * slices * count_ka))

    blocks = [u, xor_permute(u, "ja", 1)]
    for t in range(1, count_z):
        block = xor_permute(u, "ja", 2 * t)
        blocks += [block, xor_permute(block, "ja", 1)]
    places = jnp.arange(count_ja) ^ ja
    gathered = jnp.take(jnp.stack(blocks), places, axis=0).reshape(count_ja * owned, -1)
    rows = dot1(u, gathered, NT).reshape(count_ka, owned // count_ka, count_ja * owned)
    gram_two = pick(rows, ka, 0)
    for t in range(1, count_ka):
        gram_two = gram_two + xor_permute(pick(rows, ka ^ t, 0).astype(BF16), "ka", t).astype(F32)
    gram_two = gram_two * (1.0 / math.sqrt(slices * count_ka * rank_one))

    cut = factor_two.reshape(owned, count_ja, -1)
    two = [pick(cut, ja, 1)]
    two += [xor_permute(pick(cut, ja ^ b, 1), "ja", b) for b in range(1, count_ja)]
    two = jnp.take(jnp.stack(two), places, axis=0).reshape(count_ja * owned, -1)
    reduced = dot1(two, gathered, TN).reshape(-1, slices, rank_one).transpose(1, 0, 2)
    return (gram_one, gram_two, reduced)


def shards(tensor, factor_one, factor_two):
    slices, owned, width = tensor.shape
    count_ja = lax.axis_size("ja")
    count_ka = lax.axis_size("ka")
    step = width // count_ja
    columns = slices * factor_one.shape[1]
    tiled = count_ja == 8 and count_ka == 4 and factor_two.shape[1] == 256
    tiled = tiled and step % 128 == 0 and owned % 128 == 0
    tiled = tiled and step % (16 * count_ka) == 0 and owned % (16 * count_ka) == 0
    tiled = tiled and owned * 128 % (16 * columns) == 0 and columns % 128 == 0
    tiled = tiled and columns == 8 * owned and owned == 128
    return (tiled_shards if tiled else plain_shards)(tensor, factor_one, factor_two)


def solution(mesh):
    in_specs = (P("ka", "ja", None), P(), P("ja", None))
    out_specs = (P(("ja", "ka"), None), P(("ja", "ka"), None), P("ka", "ja", None))
    return jax.shard_map(shards, mesh=mesh, in_specs=in_specs, out_specs=out_specs, check_vma=False)
```
